32 devices in a mesh: dp: 1, seq: 32 (over z, y, x, core).
Axes of the slice: x: 2, y: 2, z: 4, core: 2. Of those that a mesh axis runs over, the one named last changes fastest.
Arguments:
- queries: bfloat16 [1, 8192, 2048], P('dp', 'seq'), may hold values from -40 to 40
- keys: bfloat16 [1, 8192, 2048], P('dp', 'seq'), may hold values from -40 to 40
- values: bfloat16 [1, 8192, 2048], P('dp', 'seq'), may hold values from -6 to 6
- key_gain: float32 [2048], replicated, may hold values from 0.25 to 1.75
- random_blocks: int32 [16, 128, 3], P(None, 'seq'), may hold values from 2 to 127, as said below
- out_grad: bfloat16 [1, 8192, 2048], P('dp', 'seq'), may hold values from -6 to 6
Outputs:
- attended: bfloat16 [1, 8192, 2048], P('dp', 'seq')
- query_grad: bfloat16 [1, 8192, 2048], P('dp', 'seq')
- key_grad: bfloat16 [1, 8192, 2048], P('dp', 'seq')
- value_grad: bfloat16 [1, 8192, 2048], P('dp', 'seq')
- gain_grad: float32 [2048], replicated
The draws below stay inside these ranges and needn't reach their ends.
Inputs may be any that keep to these rules, and one draw needn't show every extreme that they name: `random_blocks`: for the 4 query blocks of one device, all heads and entries together, at most 9 entries name blocks held by any one device (blocks d * 4 to d * 4 + 3), and exactly 9 name the blocks of some device.
All inputs are finite; a program needn't handle non-finite values.
Results may differ from the reference program's by a relative error of at most 0.03.
The reference program's roundings to bfloat16 on the way count: a program that leaves them out, or rounds other values in their place, can miss the bound.
Values may be sent and summed in bfloat16 or wider, within the bound.
A program may use at most 128 MiB of HBM per device.

```python
import jax
import jax.numpy as jnp
from jax import lax

HEADS = 16
HD = 128
BLOCK = 64
NG = 2
NR = 3
BATCH = 1
SEQLEN = 8192
BPD = 4
NB = 128
CAP = 9


def base_keys(key):
    raw_keys = jnp.clip(jax.random.normal(jax.random.fold_in(key, 7), (BATCH, SEQLEN, HEADS * HD), jnp.float32), -6.0, 6.0)
    return raw_keys


def draw_keys(key, part):
    return base_keys(key).astype(jnp.bfloat16)


def draw_queries(key, part):
    raw_queries = jnp.clip(jax.random.normal(jax.random.fold_in(key, 13), (BATCH, SEQLEN, HEADS * HD), jnp.float32), -6.0, 6.0)
    return raw_queries.astype(jnp.bfloat16)


def draw_random_blocks(key, part):
    owners = NB // BPD
    request_count = HEADS * BPD * NR

    def one_device(device_index):
        device_key = jax.random.fold_in(key, device_index)
        hottest = jax.random.randint(jax.random.fold_in(device_key, 1), (), 0, owners)
        ordering = jax.random.permutation(jax.random.fold_in(device_key, 2), request_count)
        owner_dev = jnp.where(ordering < CAP, hottest, (hottest + 1 + (ordering - CAP) % (owners - 1)) % owners)
        lowest = jnp.where(owner_dev == 0, NG, 0)
        local_block = jax.random.randint(jax.random.fold_in(device_key, 3), (request_count,), lowest, BPD)
        return (owner_dev * BPD + local_block).astype(jnp.int32)
    table = jax.vmap(one_device)(jnp.arange(owners))
    table = table.reshape(owners, HEADS, BPD, NR).transpose(1, 0, 2, 3).reshape(HEADS, NB, NR)
    return table.astype(jnp.int32)


def block_levels(rng, shape, pieces, low, top_value):
    loudness = 1.0
    for axis_at, parts in pieces:
        draws = jax.random.uniform(jax.random.fold_in(jax.random.fold_in(rng, 6), axis_at), (parts,), jnp.float32, low / len(pieces), top_value / len(pieces))
        loudness = loudness * jnp.repeat(jnp.exp(draws), shape[axis_at] // parts).reshape((-1,) + (1,) * (len(shape) - 1 - axis_at))
    return loudness


def centred(rng, dims, width, limit, split=(), held_as=jnp.bfloat16):
    values = jax.random.normal(rng, dims, jnp.float32) * width
    if len(split) > 0:
        values = block_levels(rng, dims, split, -0.22, 0.18) * values
    return jnp.clip(values, min=-limit, max=limit).astype(held_as)


def setup_inputs(seed: int = 0) -> dict:
    arg_keys = jax.random.split(jax.random.key(seed), 7)
    return {
        "queries": draw_queries(jax.random.fold_in(arg_keys[6], 71), 0),
        "keys": draw_keys(jax.random.fold_in(arg_keys[6], 71), 0),
        "values": centred(arg_keys[2], (BATCH, SEQLEN, HEADS * HD), 1.0, 6.0, ((1, 32),)),
        "key_gain": jnp.clip(1.0 + 0.15 * jax.random.normal(arg_keys[3], (HEADS * HD,), jnp.float32), 0.25, 1.75),
        "random_blocks": draw_random_blocks(jax.random.fold_in(arg_keys[6], 71), 0),
        "out_grad": centred(arg_keys[5], (BATCH, SEQLEN, HEADS * HD), 1.0, 6.0, ((1, 32),)),
    }


NEGATIVE = -1e30


def rounded(values_in):
    return lax.optimization_barrier(values_in.astype(jnp.bfloat16)).astype(jnp.float32)


def one_head(query_rows, key_rows, value_rows, grad_rows, table):
    score_scale = HD ** -0.5
    query_blocks = query_rows.astype(jnp.float32).reshape(NB, BLOCK, HD)
    key_blocks = key_rows.astype(jnp.float32).reshape(NB, BLOCK, HD)
    value_blocks = value_rows.astype(jnp.float32).reshape(NB, BLOCK, HD)
    grad_blocks = grad_rows.astype(jnp.float32).reshape(NB, BLOCK, HD)
    row_blocks = jnp.arange(NG, NB, dtype=jnp.int32)
    window = row_blocks[:, None] + jnp.arange(-1, 2, dtype=jnp.int32)[None, :]
    global_list = jnp.broadcast_to(jnp.arange(NG, dtype=jnp.int32)[None, :], (NB - NG, NG))
    listing = jnp.concatenate([global_list, window, table[NG:].astype(jnp.int32)], axis=1)
    valid_keys = jnp.concatenate([jnp.ones((NB - NG, NG), bool), (window >= NG) & (window < NB), jnp.ones((NB - NG, NR), bool)], axis=1)
    safe_index = jnp.clip(listing, 0, NB - 1).astype(jnp.int32)
    key_list = key_blocks[safe_index]
    value_list = value_blocks[safe_index]
    query_sel = query_blocks[NG:]
    grad_sel = grad_blocks[NG:]
    key_mask = valid_keys[:, None, :, None]
    scores = jnp.einsum("pbd,pkcd->pbkc", query_sel, key_list) * score_scale
    scores = jnp.where(key_mask, scores, NEGATIVE)
    row_top = jnp.max(scores, axis=(2, 3), keepdims=True)
    expo_vals = jnp.where(key_mask, jnp.exp(scores - row_top), 0.0)
    row_total = jnp.sum(expo_vals, axis=(2, 3), keepdims=True)
    numerator = jnp.einsum("pbkc,pkcd->pbd", rounded(expo_vals), value_list)
    sparse_out = numerator / row_total[..., 0]

    edge_count = NG * BLOCK
    edge_scores = jnp.dot(query_rows[:edge_count], key_rows.T, preferred_element_type=jnp.float32) * score_scale
    edge_top = jnp.max(edge_scores, axis=1, keepdims=True)
    edge_expo = jnp.exp(edge_scores - edge_top)
    edge_total = jnp.sum(edge_expo, axis=1, keepdims=True)
    edge_numer = jnp.dot(edge_expo.astype(jnp.bfloat16), value_rows, preferred_element_type=jnp.float32)
    edge_out = edge_numer / edge_total
    attended = jnp.concatenate([edge_out, sparse_out.reshape(-1, HD)], axis=0).astype(jnp.bfloat16)
    attended_wide = lax.optimization_barrier(attended).astype(jnp.float32)
    row_delta = jnp.sum(grad_rows.astype(jnp.float32) * attended_wide, axis=1)

    delta_sel = row_delta.reshape(NB, BLOCK)[NG:]
    weights = expo_vals / row_total
    dprobs = jnp.einsum("pbd,pkcd->pbkc", grad_sel, value_list)
    dscores = rounded(weights * (dprobs - delta_sel[:, :, None, None]) * score_scale)
    dquery_sparse = jnp.einsum("pbkc,pkcd->pbd", dscores, key_list)
    key_part = jnp.einsum("pbkc,pbd->pkcd", dscores, query_sel)
    value_part = jnp.einsum("pbkc,pbd->pkcd", rounded(weights), grad_sel)
    random_start = NG + 3
    key_part = jnp.concatenate([key_part[:, :random_start], rounded(key_part[:, random_start:])], axis=1)
    value_part = jnp.concatenate([value_part[:, :random_start], rounded(value_part[:, random_start:])], axis=1)
    flat_index = safe_index.reshape(-1)
    key_sum = jax.ops.segment_sum(key_part.reshape(-1, BLOCK, HD), flat_index, num_segments=NB)
    value_sum = jax.ops.segment_sum(value_part.reshape(-1, BLOCK, HD), flat_index, num_segments=NB)

    edge_weights = edge_expo / edge_total
    edge_dprobs = jnp.dot(grad_rows[:edge_count], value_rows.T, preferred_element_type=jnp.float32)
    edge_dscores = (edge_weights * (edge_dprobs - row_delta[:edge_count, None]) * score_scale).astype(jnp.bfloat16)
    edge_dquery = jnp.dot(edge_dscores, key_rows, preferred_element_type=jnp.float32)
    edge_dkey = jnp.dot(edge_dscores.T, query_rows[:edge_count], preferred_element_type=jnp.float32)
    edge_dvalue = jnp.dot(edge_weights.astype(jnp.bfloat16).T, grad_rows[:edge_count], preferred_element_type=jnp.float32)
    query_grad = jnp.concatenate([edge_dquery, dquery_sparse.reshape(-1, HD)], axis=0).astype(jnp.bfloat16)
    key_eff_grad = key_sum.reshape(SEQLEN, HD) + edge_dkey
    value_grad = (value_sum.reshape(SEQLEN, HD) + edge_dvalue).astype(jnp.bfloat16)
    return attended, query_grad, key_eff_grad, value_grad


def reference(queries, keys, values, key_gain, random_blocks, out_grad):
    key_eff = (keys.astype(jnp.float32) * key_gain).astype(jnp.bfloat16)

    def heads_first(array_in):
        return array_in.reshape(BATCH, SEQLEN, HEADS, HD).transpose(0, 2, 1, 3).reshape(BATCH * HEADS, SEQLEN, HD)

    def to_rows(array_in):
        return array_in.reshape(BATCH, HEADS, SEQLEN, HD).transpose(0, 2, 1, 3).reshape(BATCH, SEQLEN, HEADS * HD)

    tables = jnp.broadcast_to(random_blocks[None], (BATCH, HEADS, NB, NR)).reshape(BATCH * HEADS, NB, NR)
    results = lax.map(lambda bundle: one_head(bundle[0], bundle[1], bundle[2], bundle[3], bundle[4]),
                      (heads_first(queries), heads_first(key_eff), heads_first(values), heads_first(out_grad), tables))
    attended = to_rows(results[0])
    query_grad = to_rows(results[1])
    key_eff_grad = to_rows(results[2])
    value_grad = to_rows(results[3])
    key_grad = (key_eff_grad * key_gain).astype(jnp.bfloat16)
    gain_grad = jnp.sum(key_eff_grad * keys.astype(jnp.float32), axis=(0, 1))
    return attended, query_grad, key_grad, value_grad, gain_grad
```

```python
import functools

import jax
import jax.numpy as jnp
from jax import lax
from jax.experimental import pallas as pl
from jax.experimental.pallas import tpu as pltpu
from jax.sharding import PartitionSpec as P

HEADS = 16
HD = 128
BLOCK = 64
NG = 2
NR = 3
NK = 8
EDGE = NG * BLOCK
SCALE = HD ** (-0.5)
NEGATIVE = -1e30
VMEM = pltpu.CompilerParams(vmem_limit_bytes=56 * 1024 * 1024)
WHOLE = pl.BlockSpec(memory_space=pltpu.VMEM)


def dot_nt(a, b):
    return lax.dot_general(a, b, (((1,), (1,)), ((), ())), preferred_element_type=jnp.float32)


def dot_nn(a, b):
    return lax.dot_general(a, b, (((1,), (0,)), ((), ())), preferred_element_type=jnp.float32)


def dot_tn(a, b):
    return lax.dot_general(a, b, (((0,), (0,)), ((), ())), preferred_element_type=jnp.float32)


def passed_along(array, axis, by):
    length = lax.axis_size(axis)
    pairs = [(i, i + by) for i in range(length) if 0 <= i + by < length]
    return lax.ppermute(array, axis, pairs)


def pick_kernel(per_dev, slots, index_ref, key_ref, value_ref, out_ref):
    def step(s, carry):
        table = jnp.maximum(index_ref[s], 0)
        rows = pl.ds(pl.multiple_of(lax.rem(table, per_dev) * BLOCK, BLOCK), BLOCK)
        cols = pl.ds(pl.multiple_of(lax.div(table, per_dev) * HD, HD), HD)
        out_ref[s, :, :HD] = key_ref[rows, cols]
        out_ref[s, :, HD:] = value_ref[rows, cols]
        return carry

    lax.fori_loop(0, slots, step, 0)


def pick(index, key_eff, values, per_dev):
    slots = index.shape[0]
    return pl.pallas_call(
        functools.partial(pick_kernel, per_dev, slots),
        grid_spec=pltpu.PrefetchScalarGridSpec(
            num_scalar_prefetch=1, grid=(), in_specs=[WHOLE, WHOLE], out_specs=WHOLE
        ),
        out_shape=jax.ShapeDtypeStruct((slots, BLOCK, 2 * HD), jnp.bfloat16),
        compiler_params=VMEM,
        name="pick",
    )(index, key_eff, values)


def sparse_kernel(
    per_dev, place_ref, pos_ref, q_ref, k_ref, v_ref, g_ref, left_ref, right_ref, edge_ref,
    arrived_ref, att_ref, dq_ref, global_ref, padded_ref, send_ref,
):
    head = pl.program_id(0)
    first_block = place_ref[0]
    total_blocks = place_ref[1]

    @pl.when(head == 0)
    def _():
        send_ref[...] = jnp.zeros_like(send_ref)

    k_window = jnp.concatenate([left_ref[0], k_ref[...], right_ref[0]], axis=0)
    v_window = jnp.concatenate([left_ref[1], v_ref[...], right_ref[1]], axis=0)
    global_ref[...] = jnp.zeros_like(global_ref)
    padded_ref[...] = jnp.zeros_like(padded_ref)
    column = lax.broadcasted_iota(jnp.int32, (1, NK * BLOCK), 1)
    for p in range(per_dev):
        rows = slice(p * BLOCK, (p + 1) * BLOCK)
        block = first_block + p
        slots = [pos_ref[(head * per_dev + p) * NR + r] for r in range(NR)]
        picked = [arrived_ref[s] for s in slots]
        window = slice(p * BLOCK, (p + 3) * BLOCK)
        keys = jnp.concatenate(
            [edge_ref[1], k_window[window]] + [x[:, :HD] for x in picked], axis=0
        )
        values = jnp.concatenate(
            [edge_ref[2], v_window[window]] + [x[:, HD:] for x in picked], axis=0
        )
        listed = block - 1 - NG + column // BLOCK
        mask = (column < EDGE) | (column >= EDGE + 3 * BLOCK)
        mask = mask | ((listed >= NG) & (listed < total_blocks))
        q = q_ref[rows, :]
        g = g_ref[rows, :]
        scores = jnp.where(mask, dot_nt(q, keys) * SCALE, NEGATIVE)
        top = jnp.max(scores, axis=1, keepdims=True)
        expo = jnp.where(mask, jnp.exp(scores - top), 0.0)
        total = jnp.sum(expo, axis=1, keepdims=True)
        attended = (dot_nn(expo.astype(jnp.bfloat16), values) / total).astype(jnp.bfloat16)
        delta = jnp.sum(
            g.astype(jnp.float32) * attended.astype(jnp.float32), axis=1, keepdims=True
        )
        keep = jnp.where(block >= NG, 1.0, 0.0).astype(jnp.float32)
        weights = expo * (keep / total)
        dprobs = dot_nt(g, values)
        dscores = (weights * (dprobs - delta) * SCALE).astype(jnp.bfloat16)
        weights_b = weights.astype(jnp.bfloat16)
        att_ref[rows, :] = attended
        dq_ref[rows, :] = dot_nn(dscores, keys).astype(jnp.bfloat16)
        for part, terms in ((0, dot_tn(dscores, q)), (1, dot_tn(weights_b, g))):
            global_ref[part] += terms[:EDGE]
            padded_ref[part, window, :] += terms[EDGE : EDGE + 3 * BLOCK]
            for r in range(NR):
                start = EDGE + (3 + r) * BLOCK
                send_ref[slots[r], :, part * HD : (part + 1) * HD] = terms[
                    start : start + BLOCK
                ].astype(jnp.bfloat16)


def head_spec(rows):
    return pl.BlockSpec((rows, HD), lambda h, *_: (0, h))


def head_spec_3(parts, rows):
    return pl.BlockSpec((parts, rows, HD), lambda h, *_: (0, 0, h))


def row_spec():
    return pl.BlockSpec((1, 1, EDGE), lambda h, *_: (h, 0, 0))


def sparse(place, position, q, k, v, g, left, right, edge, arrived, per_dev):
    tok = q.shape[0]
    width = q.shape[1]
    wide = tok + 2 * BLOCK
    return pl.pallas_call(
        functools.partial(sparse_kernel, per_dev),
        grid_spec=pltpu.PrefetchScalarGridSpec(
            num_scalar_prefetch=2,
            grid=(HEADS,),
            in_specs=[head_spec(tok)] * 4
            + [head_spec_3(2, BLOCK)] * 2
            + [head_spec_3(4, EDGE), WHOLE],
            out_specs=[
                head_spec(tok),
                head_spec(tok),
                head_spec_3(2, EDGE),
                head_spec_3(2, wide),
                WHOLE,
            ],
        ),
        out_shape=[
            jax.ShapeDtypeStruct((tok, width), jnp.bfloat16),
            jax.ShapeDtypeStruct((tok, width), jnp.bfloat16),
            jax.ShapeDtypeStruct((2, EDGE, width), jnp.float32),
            jax.ShapeDtypeStruct((2, wide, width), jnp.float32),
            jax.ShapeDtypeStruct(arrived.shape, jnp.bfloat16),
        ],
        compiler_params=VMEM,
        name="sparse",
    )(place, position, q, k, v, g, left, right, edge, arrived)


def edge_top_kernel(edge_ref, k_ref, top_ref):
    scores = dot_nt(k_ref[...], edge_ref[0]) * SCALE
    top_ref[0] = jnp.max(scores, axis=0, keepdims=True)


def edge_sum_kernel(edge_ref, k_ref, v_ref, top_ref, total_ref, numer_ref):
    scores = dot_nt(k_ref[...], edge_ref[0]) * SCALE
    expo = jnp.exp(scores - top_ref[0])
    total_ref[0] = jnp.sum(expo, axis=0, keepdims=True)
    numer_ref[...] = dot_tn(expo.astype(jnp.bfloat16), v_ref[...])


def edge_grad_kernel(edge_ref, k_ref, v_ref, top_ref, total_ref, delta_ref, dq_ref, dkv_ref):
    q = edge_ref[0]
    g = edge_ref[3]
    scores = dot_nt(k_ref[...], q) * SCALE
    weights = jnp.exp(scores - top_ref[0]) / total_ref[0]
    dprobs = dot_nt(v_ref[...], g)
    dscores = (weights * (dprobs - delta_ref[0]) * SCALE).astype(jnp.bfloat16)
    dq_ref[...] = dot_tn(dscores, k_ref[...])
    dkv_ref[0] = dot_nn(dscores, q)
    dkv_ref[1] = dot_nn(weights.astype(jnp.bfloat16), g)


def edge_call(kernel, inputs, specs, outs, out_specs, name):
    return pl.pallas_call(
        kernel,
        grid=(HEADS,),
        in_specs=specs,
        out_specs=out_specs,
        out_shape=[jax.ShapeDtypeStruct(s, jnp.float32) for s in outs],
        compiler_params=VMEM,
        name=name,
    )(*inputs)


def final_kernel(
    per_dev, slots, place_ref, served_ref, returned_ref, padded_ref, local_ref, next_ref,
    prev_ref, global_ref, keys_ref, gain_ref, edq_ref, eout_ref, att_ref, dq_ref,
    att_out, dq_out, dk_out, dv_out, gain_out, acc_ref,
):
    head = pl.program_id(0)
    first_block = place_ref[0]

    @pl.when(head == 0)
    def _():
        acc_ref[...] = jnp.zeros_like(acc_ref)

        def step(s, carry):
            table = served_ref[s]

            @pl.when(table >= 0)
            def _():
                acc_ref[table] += returned_ref[s].astype(jnp.float32)

            return carry

        lax.fori_loop(0, slots, step, 0)

    gain_sum = jnp.zeros((1, HD), jnp.float32)
    for p in range(per_dev):
        rows = slice(p * BLOCK, (p + 1) * BLOCK)
        shifted = slice((p + 1) * BLOCK, (p + 2) * BLOCK)
        summed = acc_ref[head * per_dev + p]
        sums = []
        for part in range(2):
            term = padded_ref[part, shifted, :] + local_ref[part, rows, :]
            term = term + summed[:, part * HD : (part + 1) * HD]
            if p == per_dev - 1:
                term = term + next_ref[part].astype(jnp.float32)
            if p == 0:
                term = term + prev_ref[part].astype(jnp.float32)
            if p < NG:
                term = term + jnp.where(
                    first_block == 0, global_ref[part, rows, :].astype(jnp.float32), 0.0
                )
            sums.append(term)
        dk_out[rows, :] = (sums[0] * gain_ref[...]).astype(jnp.bfloat16)
        dv_out[rows, :] = sums[1].astype(jnp.bfloat16)
        gain_sum = gain_sum + jnp.sum(
            sums[0] * keys_ref[rows, :].astype(jnp.float32), axis=0, keepdims=True
        )
        if p < NG:
            is_edge = first_block == 0
            att_out[rows, :] = jnp.where(is_edge, eout_ref[rows, :], att_ref[rows, :])
            dq_out[rows, :] = jnp.where(
                is_edge, edq_ref[rows, :].astype(jnp.bfloat16), dq_ref[rows, :]
            )
        else:
            att_out[rows, :] = att_ref[rows, :]
            dq_out[rows, :] = dq_ref[rows, :]
    gain_out[...] = gain_sum


def final(place, served, returned, padded, local, nxt, prev, glob, keys, gain, edq, eout, att, dq,
          per_dev):
    tok = keys.shape[0]
    width = keys.shape[1]
    slots = served.shape[0]
    return pl.pallas_call(
        functools.partial(final_kernel, per_dev, slots),
        grid_spec=pltpu.PrefetchScalarGridSpec(
            num_scalar_prefetch=2,
            grid=(HEADS,),
            in_specs=[
                WHOLE,
                head_spec_3(2, tok + 2 * BLOCK),
                head_spec_3(2, tok),
                head_spec_3(2, BLOCK),
                head_spec_3(2, BLOCK),
                head_spec_3(2, EDGE),
                head_spec(tok),
                head_spec(1),
                head_spec(EDGE),
                head_spec(EDGE),
                head_spec(tok),
                head_spec(tok),
            ],
            out_specs=[head_spec(tok)] * 4 + [head_spec(1)],
            scratch_shapes=[pltpu.VMEM((HEADS * per_dev, BLOCK, 2 * HD), jnp.float32)],
        ),
        out_shape=[jax.ShapeDtypeStruct((tok, width), jnp.bfloat16)] * 4
        + [jax.ShapeDtypeStruct((1, width), jnp.float32)],
        compiler_params=VMEM,
        name="final",
    )(place, served, returned, padded, local, nxt, prev, glob, keys, gain, edq, eout, att, dq)


def shards(queries, keys, values, key_gain, random_blocks, out_grad):
    tok = queries.shape[1]
    width = queries.shape[2]
    per_dev = tok // BLOCK
    owners = lax.axis_size("seq")
    seq_place = lax.axis_index("seq")
    first_block = seq_place * per_dev
    place = jnp.stack([first_block, jnp.int32(owners * per_dev)]).astype(jnp.int32)
    q, v, g = queries[0], values[0], out_grad[0]
    key_eff = (keys[0].astype(jnp.float32) * key_gain).astype(jnp.bfloat16)

    request_count = HEADS * per_dev * NR
    capacity = (request_count + owners - 1) // owners + 3
    target = random_blocks.reshape(request_count)
    owner_dev = target // per_dev
    table_index = (
        jnp.arange(request_count, dtype=jnp.int32) // (per_dev * NR) * per_dev + target % per_dev
    )
    onehot = (owner_dev[:, None] == jnp.arange(owners, dtype=jnp.int32)[None, :]).astype(jnp.int32)
    before = jnp.cumsum(onehot, axis=0) - onehot
    slot_rank = jnp.sum(before * onehot, axis=1)
    position = (owner_dev * capacity + slot_rank).astype(jnp.int32)
    hit = position[:, None] == jnp.arange(owners * capacity, dtype=jnp.int32)[None, :]
    outgoing = (
        jnp.sum(jnp.where(hit, table_index[:, None] + 1, 0), axis=0).astype(jnp.int32) - 1
    ).reshape(owners, capacity)
    served = lax.all_to_all(outgoing, "seq", split_axis=0, concat_axis=0, tiled=True)
    served = served.reshape(owners * capacity)
    picked = pick(served, key_eff, v, per_dev)

    def exchange(slots):
        shaped = slots.reshape(owners, capacity, BLOCK, 2 * HD)
        moved = lax.all_to_all(shaped, "seq", split_axis=0, concat_axis=0, tiled=True)
        return moved.reshape(owners * capacity, BLOCK, 2 * HD)

    edge = jnp.stack([q[:EDGE], key_eff[:EDGE], v[:EDGE], g[:EDGE]])
    edge = lax.psum(jnp.where(seq_place == 0, edge, jnp.zeros_like(edge)), "seq")
    tails = jnp.stack([key_eff[tok - BLOCK :], v[tok - BLOCK :]])
    heads = jnp.stack([key_eff[:BLOCK], v[:BLOCK]])
    left = passed_along(tails, "seq", 1)
    right = passed_along(heads, "seq", -1)
    arrived = exchange(picked)

    rows = (HEADS, 1, EDGE)
    edge_in = head_spec_3(4, EDGE)
    (local_top,) = edge_call(
        edge_top_kernel, (edge, key_eff), [edge_in, head_spec(tok)], [rows], [row_spec()], "top"
    )
    top = lax.pmax(local_top, "seq")
    total, numer = lax.psum(
        tuple(
            edge_call(
                edge_sum_kernel,
                (edge, key_eff, v, top),
                [edge_in, head_spec(tok), head_spec(tok), row_spec()],
                [rows, (EDGE, width)],
                [row_spec(), head_spec(EDGE)],
                "sums",
            )
        ),
        "seq",
    )
    numer = numer.reshape(EDGE, HEADS, HD)
    edge_out = (numer / total[:, 0].T[:, :, None]).astype(jnp.bfloat16)
    edge_delta = jnp.sum(
        edge[3].reshape(EDGE, HEADS, HD).astype(jnp.float32) * edge_out.astype(jnp.float32), axis=2
    ).T[:, None]
    edge_out = edge_out.reshape(EDGE, width)
    edge_dq, local = edge_call(
        edge_grad_kernel,
        (edge, key_eff, v, top, total, edge_delta),
        [edge_in, head_spec(tok), head_spec(tok), row_spec(), row_spec(), row_spec()],
        [(EDGE, width), (2, tok, width)],
        [head_spec(EDGE), head_spec_3(2, tok)],
        "grads",
    )
    arrived, edge_dq, local = lax.optimization_barrier((arrived, edge_dq, local))

    att, dq, global_part, padded, send = sparse(
        place, position, q, key_eff, v, g, left, right, edge, arrived, per_dev
    )
    returned = exchange(send)
    nxt = passed_along(padded[:, :BLOCK].astype(jnp.bfloat16), "seq", -1)
    prev = passed_along(padded[:, tok + BLOCK :].astype(jnp.bfloat16), "seq", 1)
    edge_dq, global_sum = lax.psum((edge_dq, global_part), "seq")
    att, dq, dk, dv, gain_term = final(
        place, served, returned, padded, local, nxt, prev, global_sum, keys[0],
        key_gain[None], edge_dq, edge_out, att, dq, per_dev,
    )
    gain_grad = lax.psum(gain_term[0], ("dp", "seq"))
    return att[None], dq[None], dk[None], dv[None], gain_grad


def solution(mesh):
    placed = (
        P("dp", "seq", None),
        P("dp", "seq", None),
        P("dp", "seq", None),
        P(),
        P(None, "seq", None),
        P("dp", "seq", None),
    )
    return jax.shard_map(
        shards,
        mesh=mesh,
        in_specs=placed,
        out_specs=(
            P("dp", "seq", None),
            P("dp", "seq", None),
            P("dp", "seq", None),
            P("dp", "seq", None),
            P(),
        ),
        check_vma=False,
    )
```

```python
import functools

import jax
import jax.numpy as jnp
from jax import lax
from jax.experimental import pallas as pl
from jax.experimental.pallas import tpu as pltpu
from jax.sharding import PartitionSpec as P

HEADS = 16
HD = 128
BLOCK = 64
NG = 2
NR = 3
NK = 8
EDGE = NG * BLOCK
SCALE = HD ** (-0.5)
NEGATIVE = -1e30
VMEM = pltpu.CompilerParams(vmem_limit_bytes=56 * 1024 * 1024)
WHOLE = pl.BlockSpec(memory_space=pltpu.VMEM)


def dot_nt(a, b):
    return lax.dot_general(a, b, (((1,), (1,)), ((), ())), preferred_element_type=jnp.float32)


def dot_nn(a, b):
    return lax.dot_general(a, b, (((1,), (0,)), ((), ())), preferred_element_type=jnp.float32)


def dot_tn(a, b):
    return lax.dot_general(a, b, (((0,), (0,)), ((), ())), preferred_element_type=jnp.float32)


def passed_along(array, axis, by):
    length = lax.axis_size(axis)
    pairs = [(i, i + by) for i in range(length) if 0 <= i + by < length]
    return lax.ppermute(array, axis, pairs)


def pick_kernel(per_dev, slots, index_ref, key_ref, value_ref, key_out, value_out):
    def step(s, carry):
        table = jnp.maximum(index_ref[s], 0)
        rows = pl.ds(pl.multiple_of(lax.rem(table, per_dev) * BLOCK, BLOCK), BLOCK)
        cols = pl.ds(pl.multiple_of(lax.div(table, per_dev) * HD, HD), HD)
        key_out[s] = key_ref[rows, cols]
        value_out[s] = value_ref[rows, cols]
        return carry

    lax.fori_loop(0, slots, step, 0)


def pick(index, key_eff, values, per_dev):
    slots = index.shape[0]
    return pl.pallas_call(
        functools.partial(pick_kernel, per_dev, slots),
        grid_spec=pltpu.PrefetchScalarGridSpec(
            num_scalar_prefetch=1, grid=(), in_specs=[WHOLE, WHOLE], out_specs=[WHOLE, WHOLE]
        ),
        out_shape=[jax.ShapeDtypeStruct((slots, BLOCK, HD), jnp.bfloat16)] * 2,
        compiler_params=VMEM,
        name="pick",
    )(index, key_eff, values)


def listed_rows(edge_rows, window_rows, p, arrived_ref, slots):
    window = window_rows[p * BLOCK : (p + 3) * BLOCK]
    return jnp.concatenate([edge_rows, window] + [arrived_ref[s] for s in slots], axis=0)


def softmax_parts(q, keys, block, total_blocks):
    column = lax.broadcasted_iota(jnp.int32, (1, NK * BLOCK), 1)
    listed = block - 1 - NG + column // BLOCK
    mask = (column < EDGE) | (column >= EDGE + 3 * BLOCK)
    mask = mask | ((listed >= NG) & (listed < total_blocks))
    scores = jnp.where(mask, dot_nt(q, keys) * SCALE, NEGATIVE)
    top = jnp.max(scores, axis=1, keepdims=True)
    expo = jnp.where(mask, jnp.exp(scores - top), 0.0)
    total = jnp.sum(expo, axis=1, keepdims=True)
    keep = jnp.where(block >= NG, 1.0, 0.0).astype(jnp.float32)
    return expo, total, expo * (keep / total)


def scatter_terms(terms, p, slots, global_ref, padded_ref, send_ref):
    global_ref[...] += terms[:EDGE]
    padded_ref[p * BLOCK : (p + 3) * BLOCK, :] += terms[EDGE : EDGE + 3 * BLOCK]
    for r in range(NR):
        start = EDGE + (3 + r) * BLOCK
        send_ref[slots[r]] = terms[start : start + BLOCK].astype(jnp.bfloat16)


def clear(head, global_ref, padded_ref, send_ref):
    @pl.when(head == 0)
    def _():
        send_ref[...] = jnp.zeros_like(send_ref)

    global_ref[...] = jnp.zeros_like(global_ref)
    padded_ref[...] = jnp.zeros_like(padded_ref)


def value_kernel(
    per_dev, place_ref, pos_ref, q_ref, g_ref, k_ref, left_ref, right_ref, edge_ref,
    arrived_ref, global_ref, padded_ref, send_ref,
):
    head = pl.program_id(0)
    clear(head, global_ref, padded_ref, send_ref)
    k_window = jnp.concatenate([left_ref[0], k_ref[...], right_ref[0]], axis=0)
    for p in range(per_dev):
        rows = slice(p * BLOCK, (p + 1) * BLOCK)
        slots = [pos_ref[(head * per_dev + p) * NR + r] for r in range(NR)]
        keys = listed_rows(edge_ref[1], k_window, p, arrived_ref, slots)
        _, _, weights = softmax_parts(q_ref[rows, :], keys, place_ref[0] + p, place_ref[1])
        terms = dot_tn(weights.astype(jnp.bfloat16), g_ref[rows, :])
        scatter_terms(terms, p, slots, global_ref, padded_ref, send_ref)


def key_kernel(
    per_dev, place_ref, pos_ref, q_ref, g_ref, k_ref, left_ref, right_ref, edge_ref,
    arrived_ref, v_ref, arrived_v_ref, global_ref, padded_ref, send_ref, att_ref, dq_ref,
):
    head = pl.program_id(0)
    clear(head, global_ref, padded_ref, send_ref)
    k_window = jnp.concatenate([left_ref[0], k_ref[...], right_ref[0]], axis=0)
    v_window = jnp.concatenate([left_ref[1], v_ref[...], right_ref[1]], axis=0)
    for p in range(per_dev):
        rows = slice(p * BLOCK, (p + 1) * BLOCK)
        slots = [pos_ref[(head * per_dev + p) * NR + r] for r in range(NR)]
        keys = listed_rows(edge_ref[1], k_window, p, arrived_ref, slots)
        values = listed_rows(edge_ref[2], v_window, p, arrived_v_ref, slots)
        q = q_ref[rows, :]
        g = g_ref[rows, :]
        expo, total, weights = softmax_parts(q, keys, place_ref[0] + p, place_ref[1])
        attended = (dot_nn(expo.astype(jnp.bfloat16), values) / total).astype(jnp.bfloat16)
        delta = jnp.sum(
            g.astype(jnp.float32) * attended.astype(jnp.float32), axis=1, keepdims=True
        )
        dscores = (weights * (dot_nt(g, values) - delta) * SCALE).astype(jnp.bfloat16)
        att_ref[rows, :] = attended
        dq_ref[rows, :] = dot_nn(dscores, keys).astype(jnp.bfloat16)
        scatter_terms(dot_tn(dscores, q), p, slots, global_ref, padded_ref, send_ref)


def head_spec(rows):
    return pl.BlockSpec((rows, HD), lambda h, *_: (0, h))


def head_spec_3(parts, rows):
    return pl.BlockSpec((parts, rows, HD), lambda h, *_: (0, 0, h))


def row_spec():
    return pl.BlockSpec((1, 1, EDGE), lambda h, *_: (h, 0, 0))


def sparse(kernel, place, position, inputs, more, per_dev, outs, name):
    q = inputs[0]
    tok = q.shape[0]
    width = q.shape[1]
    wide = tok + 2 * BLOCK
    slots = inputs[6].shape
    return pl.pallas_call(
        functools.partial(kernel, per_dev),
        grid_spec=pltpu.PrefetchScalarGridSpec(
            num_scalar_prefetch=2,
            grid=(HEADS,),
            in_specs=[head_spec(tok)] * 3
            + [head_spec_3(2, BLOCK)] * 2
            + [head_spec_3(4, EDGE), WHOLE]
            + [head_spec(tok), WHOLE][: len(more)],
            out_specs=[head_spec(EDGE), head_spec(wide), WHOLE] + [head_spec(tok)] * outs,
        ),
        out_shape=[
            jax.ShapeDtypeStruct((EDGE, width), jnp.float32),
            jax.ShapeDtypeStruct((wide, width), jnp.float32),
            jax.ShapeDtypeStruct(slots, jnp.bfloat16),
        ]
        + [jax.ShapeDtypeStruct((tok, width), jnp.bfloat16)] * outs,
        compiler_params=VMEM,
        name=name,
    )(place, position, *inputs, *more)


def edge_sum_kernel(edge_ref, k_ref, v_ref, top_ref, total_ref, numer_ref):
    scores = dot_nt(k_ref[...], edge_ref[0]) * SCALE
    top = jnp.max(scores, axis=0, keepdims=True)
    expo = jnp.exp(scores - top)
    top_ref[0] = top
    total_ref[0] = jnp.sum(expo, axis=0, keepdims=True)
    numer_ref[...] = dot_tn(expo.astype(jnp.bfloat16), v_ref[...])


def edge_grad_kernel(edge_ref, k_ref, v_ref, top_ref, total_ref, delta_ref, dq_ref, dkv_ref):
    q = edge_ref[0]
    g = edge_ref[3]
    scores = dot_nt(k_ref[...], q) * SCALE
    weights = jnp.exp(scores - top_ref[0]) / total_ref[0]
    dprobs = dot_nt(v_ref[...], g)
    dscores = (weights * (dprobs - delta_ref[0]) * SCALE).astype(jnp.bfloat16)
    dq_ref[...] = dot_tn(dscores, k_ref[...])
    dkv_ref[0] = dot_nn(dscores, q)
    dkv_ref[1] = dot_nn(weights.astype(jnp.bfloat16), g)


def edge_call(kernel, inputs, specs, outs, out_specs, name):
    return pl.pallas_call(
        kernel,
        grid=(HEADS,),
        in_specs=specs,
        out_specs=out_specs,
        out_shape=[jax.ShapeDtypeStruct(s, jnp.float32) for s in outs],
        compiler_params=VMEM,
        name=name,
    )(*inputs)


def sum_terms(
    per_dev, place_ref, served_ref, returned_ref, padded_ref, local_ref, next_ref, prev_ref,
    global_ref, acc_ref,
):
    head = pl.program_id(0)

    @pl.when(head == 0)
    def _():
        acc_ref[...] = jnp.zeros_like(acc_ref)

        def step(s, carry):
            table = served_ref[s]

            @pl.when(table >= 0)
            def _():
                acc_ref[table] += returned_ref[s].astype(jnp.float32)

            return carry

        lax.fori_loop(0, returned_ref.shape[0], step, 0)

    sums = []
    for p in range(per_dev):
        rows = slice(p * BLOCK, (p + 1) * BLOCK)
        shifted = slice((p + 1) * BLOCK, (p + 2) * BLOCK)
        term = padded_ref[shifted, :] + local_ref[0, rows, :] + acc_ref[head * per_dev + p]
        if p == per_dev - 1:
            term = term + next_ref[...].astype(jnp.float32)
        if p == 0:
            term = term + prev_ref[...].astype(jnp.float32)
        if p < NG:
            term = term + jnp.where(place_ref[0] == 0, global_ref[rows, :], 0.0)
        sums.append(term)
    return sums


def final_value_kernel(
    per_dev, place_ref, served_ref, returned_ref, padded_ref, local_ref, next_ref, prev_ref,
    global_ref, dv_out, acc_ref,
):
    sums = sum_terms(
        per_dev, place_ref, served_ref, returned_ref, padded_ref, local_ref, next_ref, prev_ref,
        global_ref, acc_ref,
    )
    for p in range(per_dev):
        dv_out[p * BLOCK : (p + 1) * BLOCK, :] = sums[p].astype(jnp.bfloat16)


def final_key_kernel(
    per_dev, place_ref, served_ref, returned_ref, padded_ref, local_ref, next_ref, prev_ref,
    global_ref, keys_ref, gain_ref, edq_ref, eout_ref, att_ref, dq_ref,
    dk_out, att_out, dq_out, gain_out, acc_ref,
):
    sums = sum_terms(
        per_dev, place_ref, served_ref, returned_ref, padded_ref, local_ref, next_ref, prev_ref,
        global_ref, acc_ref,
    )
    is_edge = place_ref[0] == 0
    gain_sum = jnp.zeros((1, HD), jnp.float32)
    for p in range(per_dev):
        rows = slice(p * BLOCK, (p + 1) * BLOCK)
        dk_out[rows, :] = (sums[p] * gain_ref[...]).astype(jnp.bfloat16)
        gain_sum = gain_sum + jnp.sum(
            sums[p] * keys_ref[rows, :].astype(jnp.float32), axis=0, keepdims=True
        )
        if p < NG:
            att_out[rows, :] = jnp.where(is_edge, eout_ref[rows, :], att_ref[rows, :])
            dq_out[rows, :] = jnp.where(
                is_edge, edq_ref[rows, :].astype(jnp.bfloat16), dq_ref[rows, :]
            )
        else:
            att_out[rows, :] = att_ref[rows, :]
            dq_out[rows, :] = dq_ref[rows, :]
    gain_out[...] = gain_sum


def final(kernel, part, place, served, inputs, more, per_dev, name):
    tok = inputs[2].shape[1]
    width = inputs[2].shape[2]
    more_specs = [
        head_spec(tok), head_spec(1), head_spec(EDGE), head_spec(EDGE), head_spec(tok),
        head_spec(tok),
    ]
    full = jax.ShapeDtypeStruct((tok, width), jnp.bfloat16)
    outs = [full] if not more else [full] * 3 + [jax.ShapeDtypeStruct((1, width), jnp.float32)]
    return pl.pallas_call(
        functools.partial(kernel, per_dev),
        grid_spec=pltpu.PrefetchScalarGridSpec(
            num_scalar_prefetch=2,
            grid=(HEADS,),
            in_specs=[
                WHOLE,
                head_spec(tok + 2 * BLOCK),
                pl.BlockSpec((1, tok, HD), lambda h, *_: (part, 0, h)),
                head_spec(BLOCK),
                head_spec(BLOCK),
                head_spec(EDGE),
            ]
            + more_specs[: len(more)],
            out_specs=[head_spec(x.shape[0]) for x in outs],
            scratch_shapes=[pltpu.VMEM((HEADS * per_dev, BLOCK, HD), jnp.float32)],
        ),
        out_shape=outs,
        compiler_params=VMEM,
        name=name,
    )(place, served, *inputs, *more)


def shards(queries, keys, values, key_gain, random_blocks, out_grad):
    tok = queries.shape[1]
    width = queries.shape[2]
    per_dev = tok // BLOCK
    owners = lax.axis_size("seq")
    seq_place = lax.axis_index("seq")
    first_block = seq_place * per_dev
    place = jnp.stack([first_block, jnp.int32(owners * per_dev)]).astype(jnp.int32)
    q, v, g = queries[0], values[0], out_grad[0]
    key_eff = (keys[0].astype(jnp.float32) * key_gain).astype(jnp.bfloat16)

    request_count = HEADS * per_dev * NR
    capacity = (request_count + owners - 1) // owners + 3
    target = random_blocks.reshape(request_count)
    owner_dev = target // per_dev
    table_index = (
        jnp.arange(request_count, dtype=jnp.int32) // (per_dev * NR) * per_dev + target % per_dev
    )
    onehot = (owner_dev[:, None] == jnp.arange(owners, dtype=jnp.int32)[None, :]).astype(jnp.int32)
    before = jnp.cumsum(onehot, axis=0) - onehot
    slot_rank = jnp.sum(before * onehot, axis=1)
    position = (owner_dev * capacity + slot_rank).astype(jnp.int32)
    hit = position[:, None] == jnp.arange(owners * capacity, dtype=jnp.int32)[None, :]
    outgoing = (
        jnp.sum(jnp.where(hit, table_index[:, None] + 1, 0), axis=0).astype(jnp.int32) - 1
    ).reshape(owners, capacity)
    served = lax.all_to_all(outgoing, "seq", split_axis=0, concat_axis=0, tiled=True)
    served = served.reshape(owners * capacity)
    picked_k, picked_v = pick(served, key_eff, v, per_dev)

    def exchange(slots):
        shaped = slots.reshape(owners, capacity, BLOCK, HD)
        moved = lax.all_to_all(shaped, "seq", split_axis=0, concat_axis=0, tiled=True)
        return moved.reshape(owners * capacity, BLOCK, HD)

    def to_all(array):
        spread = jnp.broadcast_to(array[None], (owners,) + array.shape)
        return lax.all_to_all(spread, "seq", split_axis=0, concat_axis=0, tiled=True)

    edge = jnp.stack([q[:EDGE], key_eff[:EDGE], v[:EDGE], g[:EDGE]])
    edge = lax.psum(jnp.where(seq_place == 0, edge, jnp.zeros_like(edge)), "seq")
    tails = jnp.stack([key_eff[tok - BLOCK :], v[tok - BLOCK :]])
    heads = jnp.stack([key_eff[:BLOCK], v[:BLOCK]])
    left = passed_along(tails, "seq", 1)
    right = passed_along(heads, "seq", -1)
    arrived_k = exchange(picked_k)
    picked_v, arrived_k = lax.optimization_barrier((picked_v, arrived_k))
    arrived_v = exchange(picked_v)

    stat = (HEADS, 1, EDGE)
    edge_in = head_spec_3(4, EDGE)
    top, total, numer = edge_call(
        edge_sum_kernel,
        (edge, key_eff, v),
        [edge_in, head_spec(tok), head_spec(tok)],
        [stat, stat, (EDGE, width)],
        [row_spec(), row_spec(), head_spec(EDGE)],
        "sums",
    )
    share = EDGE // owners
    stats = jnp.concatenate([top[:, 0].T, total[:, 0].T], axis=1)
    stats = jnp.pad(stats, ((0, 0), (0, HD - 2 * HEADS)))
    parts = jnp.concatenate([numer, stats], axis=1).reshape(owners, share, width + HD)

    base = [q, g, key_eff, left, right, edge, arrived_k]
    value_global, value_padded, send_v = sparse(
        value_kernel, place, position, base, [], per_dev, 0, "value_terms"
    )

    parts = lax.all_to_all(parts, "seq", split_axis=0, concat_axis=0, tiled=True)
    parts, send_v = lax.optimization_barrier((parts, send_v))
    tops = parts[:, :, width : width + HEADS]
    top_row = jnp.max(tops, axis=0)
    factor = jnp.exp(tops - top_row[None])
    total_row = jnp.sum(factor * parts[:, :, width + HEADS : width + 2 * HEADS], axis=0)
    numer_row = jnp.sum(
        parts[:, :, :width].reshape(owners, share, HEADS, HD) * factor[..., None], axis=0
    )
    out_row = (numer_row / total_row[..., None]).astype(jnp.bfloat16)
    grad_row = lax.dynamic_slice_in_dim(edge[3], seq_place * share, share, axis=0)
    grad_row = grad_row.reshape(share, HEADS, HD).astype(jnp.float32)
    delta_row = jnp.sum(grad_row * out_row.astype(jnp.float32), axis=2)
    row_stats = to_all(jnp.concatenate([top_row, total_row, delta_row], axis=1))
    row_stats = row_stats.reshape(EDGE, 3, HEADS).transpose(1, 2, 0)[:, :, None]
    edge_out = lax.all_gather(out_row.reshape(share, width), "seq", axis=0, tiled=True)

    arrived_v, send_v = lax.optimization_barrier((arrived_v, send_v))
    returned_v = exchange(send_v)
    key_global, key_padded, send_k, att, dq = sparse(
        key_kernel, place, position, base, [v, arrived_v], per_dev, 2, "key_terms"
    )
    row_stats, send_k = lax.optimization_barrier((row_stats, send_k))
    value_global = lax.psum(value_global, "seq")
    edge_dq, local = edge_call(
        edge_grad_kernel,
        (edge, key_eff, v, row_stats[0], row_stats[1], row_stats[2]),
        [edge_in, head_spec(tok), head_spec(tok), row_spec(), row_spec(), row_spec()],
        [(EDGE, width), (2, tok, width)],
        [head_spec(EDGE), head_spec_3(2, tok)],
        "grads",
    )
    send_k, returned_v, value_global = lax.optimization_barrier((send_k, returned_v, value_global))
    returned_k = exchange(send_k)

    def neighbours(padded):
        nxt = passed_along(padded[:BLOCK].astype(jnp.bfloat16), "seq", -1)
        prev = passed_along(padded[tok + BLOCK :].astype(jnp.bfloat16), "seq", 1)
        return nxt, prev

    edge_dq, key_global = lax.psum((edge_dq, key_global), "seq")
    (dv,) = final(
        final_value_kernel, 1, place, served,
        (returned_v, value_padded, local, *neighbours(value_padded), value_global), (),
        per_dev, "final_value",
    )
    returned_k, dv = lax.optimization_barrier((returned_k, dv))
    dk, att, dq, gain_term = final(
        final_key_kernel, 0, place, served,
        (returned_k, key_padded, local, *neighbours(key_padded), key_global),
        (keys[0], key_gain[None], edge_dq, edge_out, att, dq), per_dev, "final_key",
    )
    gain_grad = lax.psum(jnp.sum(to_all(gain_term), axis=(0, 1)), "dp")
    return att[None], dq[None], dk[None], dv[None], gain_grad


def solution(mesh):
    placed = (
        P("dp", "seq", None),
        P("dp", "seq", None),
        P("dp", "seq", None),
        P(),
        P(None, "seq", None),
        P("dp", "seq", None),
    )
    return jax.shard_map(
        shards,
        mesh=mesh,
        in_specs=placed,
        out_specs=(
            P("dp", "seq", None),
            P("dp", "seq", None),
            P("dp", "seq", None),
            P("dp", "seq", None),
            P(),
        ),
        check_vma=False,
    )
```

```python
import functools

import jax
import jax.numpy as jnp
from jax import lax
from jax.experimental import pallas as pl
from jax.experimental.pallas import tpu as pltpu
from jax.sharding import PartitionSpec as P

HEADS = 16
HD = 128
BLOCK = 64
NG = 2
NR = 3
NK = 8
EDGE = NG * BLOCK
SCALE = HD ** (-0.5)
NEGATIVE = -1e30
VMEM = pltpu.CompilerParams(vmem_limit_bytes=56 * 1024 * 1024)
WHOLE = pl.BlockSpec(memory_space=pltpu.VMEM)


def dot_nt(a, b):
    return lax.dot_general(a, b, (((1,), (1,)), ((), ())), preferred_element_type=jnp.float32)


def dot_nn(a, b):
    return lax.dot_general(a, b, (((1,), (0,)), ((), ())), preferred_element_type=jnp.float32)


def dot_tn(a, b):
    return lax.dot_general(a, b, (((0,), (0,)), ((), ())), preferred_element_type=jnp.float32)


def passed_along(array, axis, by):
    length = lax.axis_size(axis)
    pairs = [(i, i + by) for i in range(length) if 0 <= i + by < length]
    return lax.ppermute(array, axis, pairs)


def on(device):
    return dict(device_id={"seq": device}, device_id_type=pl.DeviceIdType.MESH)


def spread_kernel(count, in_ref, out_ref, send_sem, recv_sem):
    me = lax.axis_index("seq")
    children = (
        ((lax.rem(me, 8) == 0) & (me + 8 < count), 8),
        (lax.rem(me, 8) == 0, 4),
        (lax.rem(me, 4) == 0, 2),
        (lax.rem(me, 2) == 0, 1),
    )
    near = jnp.where(lax.rem(me, 4) == 2, me - 2, jnp.where(lax.rem(me, 8) == 4, me - 4, me - 8))
    parent = jnp.where(lax.rem(me, 2) == 1, me - 1, near)
    barrier = pltpu.get_barrier_semaphore()
    greeted = jnp.where(me > 0, 1, 0)
    for there, step in children:
        greeted = greeted + jnp.where(there, 1, 0)

        @pl.when(there)
        def _():
            pl.semaphore_signal(barrier, inc=1, **on(me + step))

    @pl.when(me > 0)
    def _():
        pl.semaphore_signal(barrier, inc=1, **on(parent))

    pl.semaphore_wait(barrier, greeted)

    @pl.when(me == 0)
    def _():
        out_ref[...] = in_ref[...]

    def copy(c, i, device):
        return pltpu.make_async_remote_copy(
            src_ref=out_ref.at[c],
            dst_ref=out_ref.at[c],
            send_sem=send_sem.at[i, c],
            recv_sem=recv_sem.at[c],
            **on(device),
        )

    def forward(c, carry):
        @pl.when(me > 0)
        def _():
            copy(c, 0, parent).wait_recv()

        for i, (there, step) in enumerate(children):

            @pl.when(there)
            def _():
                copy(c, i, me + step).start()

        return carry

    def finish(c, carry):
        for i, (there, step) in enumerate(children):

            @pl.when(there)
            def _():
                copy(c, i, me + step).wait_send()

        return carry

    lax.fori_loop(0, out_ref.shape[0], forward, 0)
    lax.fori_loop(0, out_ref.shape[0], finish, 0)


def spread(array, count):
    chunks = array.shape[0]
    return pl.pallas_call(
        functools.partial(spread_kernel, count),
        in_specs=[WHOLE],
        out_specs=WHOLE,
        out_shape=jax.ShapeDtypeStruct(array.shape, array.dtype),
        scratch_shapes=[
            pltpu.SemaphoreType.DMA((4, chunks)),
            pltpu.SemaphoreType.DMA((chunks,)),
        ],
        compiler_params=pltpu.CompilerParams(
            collective_id=0, has_side_effects=True, vmem_limit_bytes=32 * 1024 * 1024
        ),
        name="spread",
    )(array)


def collect_kernel(count, in_ref, out_ref, send_sem, recv_sem):
    me = lax.axis_index("seq")
    barrier = pltpu.get_barrier_semaphore()

    def copy(device):
        return pltpu.make_async_remote_copy(
            src_ref=in_ref,
            dst_ref=out_ref.at[device],
            send_sem=send_sem,
            recv_sem=recv_sem.at[device],
            **on(0),
        )

    @pl.when(me == 0)
    def _():
        def greet(d, carry):
            pl.semaphore_signal(barrier, inc=1, **on(d))
            return carry

        lax.fori_loop(1, count, greet, 0)
        pl.semaphore_wait(barrier, count - 1)
        out_ref[0] = in_ref[...]

        def receive(d, carry):
            copy(d).wait_recv()
            return carry

        lax.fori_loop(1, count, receive, 0)

    @pl.when(me > 0)
    def _():
        pl.semaphore_signal(barrier, inc=1, **on(0))
        pl.semaphore_wait(barrier, 1)
        copy(me).start()
        copy(me).wait_send()


def collect(piece, count):
    return pl.pallas_call(
        functools.partial(collect_kernel, count),
        in_specs=[WHOLE],
        out_specs=WHOLE,
        out_shape=jax.ShapeDtypeStruct((count,) + piece.shape, piece.dtype),
        scratch_shapes=[pltpu.SemaphoreType.DMA, pltpu.SemaphoreType.DMA((count,))],
        compiler_params=pltpu.CompilerParams(
            collective_id=1, has_side_effects=True, vmem_limit_bytes=32 * 1024 * 1024
        ),
        name="collect",
    )(piece)


def pick_kernel(per_dev, slots, index_ref, key_ref, value_ref, key_out, value_out):
    def step(s, carry):
        table = jnp.maximum(index_ref[s], 0)
        rows = pl.ds(pl.multiple_of(lax.rem(table, per_dev) * BLOCK, BLOCK), BLOCK)
        cols = pl.ds(pl.multiple_of(lax.div(table, per_dev) * HD, HD), HD)
        key_out[s] = key_ref[rows, cols]
        value_out[s] = value_ref[rows, cols]
        return carry

    lax.fori_loop(0, slots, step, 0)


def pick(index, key_eff, values, per_dev):
    slots = index.shape[0]
    return pl.pallas_call(
        functools.partial(pick_kernel, per_dev, slots),
        grid_spec=pltpu.PrefetchScalarGridSpec(
            num_scalar_prefetch=1, grid=(), in_specs=[WHOLE, WHOLE], out_specs=[WHOLE, WHOLE]
        ),
        out_shape=[jax.ShapeDtypeStruct((slots, BLOCK, HD), jnp.bfloat16)] * 2,
        compiler_params=VMEM,
        name="pick",
    )(index, key_eff, values)


def listed_rows(edge_rows, window_rows, p, arrived_ref, slots):
    window = window_rows[p * BLOCK : (p + 3) * BLOCK]
    return jnp.concatenate([edge_rows, window] + [arrived_ref[s] for s in slots], axis=0)


def softmax_parts(q, keys, block, total_blocks):
    column = lax.broadcasted_iota(jnp.int32, (1, NK * BLOCK), 1)
    listed = block - 1 - NG + column // BLOCK
    mask = (column < EDGE) | (column >= EDGE + 3 * BLOCK)
    mask = mask | ((listed >= NG) & (listed < total_blocks))
    scores = jnp.where(mask, dot_nt(q, keys) * SCALE, NEGATIVE)
    top = jnp.max(scores, axis=1, keepdims=True)
    expo = jnp.where(mask, jnp.exp(scores - top), 0.0)
    total = jnp.sum(expo, axis=1, keepdims=True)
    keep = jnp.where(block >= NG, 1.0, 0.0).astype(jnp.float32)
    return expo, total, expo * (keep / total)


def scatter_terms(terms, p, slots, global_ref, padded_ref, send_ref):
    global_ref[...] += terms[:EDGE]
    padded_ref[p * BLOCK : (p + 3) * BLOCK, :] += terms[EDGE : EDGE + 3 * BLOCK]
    for r in range(NR):
        start = EDGE + (3 + r) * BLOCK
        send_ref[slots[r]] = terms[start : start + BLOCK].astype(jnp.bfloat16)


def clear(head, global_ref, padded_ref, send_ref):
    @pl.when(head == 0)
    def _():
        send_ref[...] = jnp.zeros_like(send_ref)

    global_ref[...] = jnp.zeros_like(global_ref)
    padded_ref[...] = jnp.zeros_like(padded_ref)


def value_kernel(
    per_dev, place_ref, pos_ref, q_ref, g_ref, k_ref, left_ref, right_ref, edge_ref,
    arrived_ref, global_ref, padded_ref, send_ref,
):
    head = pl.program_id(0)
    clear(head, global_ref, padded_ref, send_ref)
    k_window = jnp.concatenate([left_ref[0], k_ref[...], right_ref[0]], axis=0)
    for p in range(per_dev):
        rows = slice(p * BLOCK, (p + 1) * BLOCK)
        slots = [pos_ref[(head * per_dev + p) * NR + r] for r in range(NR)]
        keys = listed_rows(edge_ref[1], k_window, p, arrived_ref, slots)
        _, _, weights = softmax_parts(q_ref[rows, :], keys, place_ref[0] + p, place_ref[1])
        terms = dot_tn(weights.astype(jnp.bfloat16), g_ref[rows, :])
        scatter_terms(terms, p, slots, global_ref, padded_ref, send_ref)


def key_kernel(
    per_dev, place_ref, pos_ref, q_ref, g_ref, k_ref, left_ref, right_ref, edge_ref,
    arrived_ref, v_ref, arrived_v_ref, global_ref, padded_ref, send_ref, att_ref, dq_ref,
):
    head = pl.program_id(0)
    clear(head, global_ref, padded_ref, send_ref)
    k_window = jnp.concatenate([left_ref[0], k_ref[...], right_ref[0]], axis=0)
    v_window = jnp.concatenate([left_ref[1], v_ref[...], right_ref[1]], axis=0)
    for p in range(per_dev):
        rows = slice(p * BLOCK, (p + 1) * BLOCK)
        slots = [pos_ref[(head * per_dev + p) * NR + r] for r in range(NR)]
        keys = listed_rows(edge_ref[1], k_window, p, arrived_ref, slots)
        values = listed_rows(edge_ref[2], v_window, p, arrived_v_ref, slots)
        q = q_ref[rows, :]
        g = g_ref[rows, :]
        expo, total, weights = softmax_parts(q, keys, place_ref[0] + p, place_ref[1])
        attended = (dot_nn(expo.astype(jnp.bfloat16), values) / total).astype(jnp.bfloat16)
        delta = jnp.sum(
            g.astype(jnp.float32) * attended.astype(jnp.float32), axis=1, keepdims=True
        )
        dscores = (weights * (dot_nt(g, values) - delta) * SCALE).astype(jnp.bfloat16)
        att_ref[rows, :] = attended
        dq_ref[rows, :] = dot_nn(dscores, keys).astype(jnp.bfloat16)
        scatter_terms(dot_tn(dscores, q), p, slots, global_ref, padded_ref, send_ref)


def head_spec(rows):
    return pl.BlockSpec((rows, HD), lambda h, *_: (0, h))


def head_spec_3(parts, rows):
    return pl.BlockSpec((parts, rows, HD), lambda h, *_: (0, 0, h))


def row_spec():
    return pl.BlockSpec((1, 1, EDGE), lambda h, *_: (h, 0, 0))


def sparse(kernel, place, position, inputs, more, per_dev, outs, name):
    q = inputs[0]
    tok = q.shape[0]
    width = q.shape[1]
    wide = tok + 2 * BLOCK
    slots = inputs[6].shape
    return pl.pallas_call(
        functools.partial(kernel, per_dev),
        grid_spec=pltpu.PrefetchScalarGridSpec(
            num_scalar_prefetch=2,
            grid=(HEADS,),
            in_specs=[head_spec(tok)] * 3
            + [head_spec_3(2, BLOCK)] * 2
            + [head_spec_3(4, EDGE), WHOLE]
            + [head_spec(tok), WHOLE][: len(more)],
            out_specs=[head_spec(EDGE), head_spec(wide), WHOLE] + [head_spec(tok)] * outs,
        ),
        out_shape=[
            jax.ShapeDtypeStruct((EDGE, width), jnp.float32),
            jax.ShapeDtypeStruct((wide, width), jnp.float32),
            jax.ShapeDtypeStruct(slots, jnp.bfloat16),
        ]
        + [jax.ShapeDtypeStruct((tok, width), jnp.bfloat16)] * outs,
        compiler_params=VMEM,
        name=name,
    )(place, position, *inputs, *more)


def edge_sum_kernel(edge_ref, k_ref, v_ref, top_ref, total_ref, numer_ref):
    scores = dot_nt(k_ref[...], edge_ref[0]) * SCALE
    top = jnp.max(scores, axis=0, keepdims=True)
    expo = jnp.exp(scores - top)
    top_ref[0] = top
    total_ref[0] = jnp.sum(expo, axis=0, keepdims=True)
    numer_ref[...] = dot_tn(expo.astype(jnp.bfloat16), v_ref[...])


def edge_grad_kernel(edge_ref, k_ref, v_ref, top_ref, total_ref, delta_ref, dq_ref, dkv_ref):
    q = edge_ref[0]
    g = edge_ref[3]
    scores = dot_nt(k_ref[...], q) * SCALE
    weights = jnp.exp(scores - top_ref[0]) / total_ref[0]
    dprobs = dot_nt(v_ref[...], g)
    dscores = (weights * (dprobs - delta_ref[0]) * SCALE).astype(jnp.bfloat16)
    dq_ref[...] = dot_tn(dscores, k_ref[...])
    dkv_ref[0] = dot_nn(dscores, q)
    dkv_ref[1] = dot_nn(weights.astype(jnp.bfloat16), g)


def edge_call(kernel, inputs, specs, outs, out_specs, name):
    return pl.pallas_call(
        kernel,
        grid=(HEADS,),
        in_specs=specs,
        out_specs=out_specs,
        out_shape=[jax.ShapeDtypeStruct(s, jnp.float32) for s in outs],
        compiler_params=VMEM,
        name=name,
    )(*inputs)


def sum_terms(
    per_dev, capacity, place_ref, served_ref, returned_ref, padded_ref, local_ref, next_ref,
    prev_ref, global_ref, acc_ref,
):
    head = pl.program_id(0)

    @pl.when(head == 0)
    def _():
        acc_ref[...] = jnp.zeros_like(acc_ref)

        def step(s, carry):
            table = served_ref[s]

            @pl.when(table >= 0)
            def _():
                block = returned_ref[lax.div(s, capacity), lax.rem(s, capacity)]
                acc_ref[table] += block.astype(jnp.float32)

            return carry

        lax.fori_loop(0, returned_ref.shape[0] * capacity, step, 0)

    sums = []
    for p in range(per_dev):
        rows = slice(p * BLOCK, (p + 1) * BLOCK)
        shifted = slice((p + 1) * BLOCK, (p + 2) * BLOCK)
        term = padded_ref[shifted, :] + local_ref[0, rows, :] + acc_ref[head * per_dev + p]
        if p == per_dev - 1:
            term = term + next_ref[...].astype(jnp.float32)
        if p == 0:
            term = term + prev_ref[...].astype(jnp.float32)
        if global_ref is not None and p < NG:
            whole = global_ref[rows, :].astype(jnp.float32)
            term = term + jnp.where(place_ref[0] == 0, whole, 0.0)
        sums.append(term)
    return sums


def final_value_kernel(
    per_dev, capacity, place_ref, served_ref, returned_ref, padded_ref, local_ref, next_ref,
    prev_ref, dv_out, acc_ref,
):
    sums = sum_terms(
        per_dev, capacity, place_ref, served_ref, returned_ref, padded_ref, local_ref, next_ref,
        prev_ref, None, acc_ref,
    )
    for p in range(per_dev):
        dv_out[p * BLOCK : (p + 1) * BLOCK, :] = sums[p]


def final_key_kernel(
    per_dev, capacity, place_ref, served_ref, returned_ref, padded_ref, local_ref, next_ref,
    prev_ref, gk_ref, gv_ref, edq_ref, eout_ref, keys_ref, gain_ref, att_ref, dq_ref, dv_ref,
    dk_out, att_out, dq_out, dv_out, gain_out, acc_ref,
):
    sums = sum_terms(
        per_dev, capacity, place_ref, served_ref, returned_ref, padded_ref, local_ref, next_ref,
        prev_ref, gk_ref, acc_ref,
    )
    is_edge = place_ref[0] == 0
    gain_sum = jnp.zeros((1, HD), jnp.float32)
    for p in range(per_dev):
        rows = slice(p * BLOCK, (p + 1) * BLOCK)
        dk_out[rows, :] = (sums[p] * gain_ref[...]).astype(jnp.bfloat16)
        gain_sum = gain_sum + jnp.sum(
            sums[p] * keys_ref[rows, :].astype(jnp.float32), axis=0, keepdims=True
        )
        if p < NG:
            att_out[rows, :] = jnp.where(is_edge, eout_ref[rows, :], att_ref[rows, :])
            dq_out[rows, :] = jnp.where(is_edge, edq_ref[rows, :], dq_ref[rows, :])
            whole = jnp.where(is_edge, gv_ref[rows, :].astype(jnp.float32), 0.0)
            dv_out[rows, :] = (dv_ref[rows, :] + whole).astype(jnp.bfloat16)
        else:
            dv_out[rows, :] = dv_ref[rows, :].astype(jnp.bfloat16)
            att_out[rows, :] = att_ref[rows, :]
            dq_out[rows, :] = dq_ref[rows, :]
    gain_out[...] = gain_sum


def final(kernel, part, capacity, place, served, inputs, more, per_dev, name):
    tok = inputs[2].shape[1]
    width = inputs[2].shape[2]
    more_specs = [head_spec(x.shape[0]) for x in more]
    outs = [jax.ShapeDtypeStruct((tok, width), jnp.float32)]
    if more:
        outs = [jax.ShapeDtypeStruct((tok, width), jnp.bfloat16)] * 4
        outs = outs + [jax.ShapeDtypeStruct((1, width), jnp.float32)]
    return pl.pallas_call(
        functools.partial(kernel, per_dev, capacity),
        grid_spec=pltpu.PrefetchScalarGridSpec(
            num_scalar_prefetch=2,
            grid=(HEADS,),
            in_specs=[
                WHOLE,
                head_spec(tok + 2 * BLOCK),
                pl.BlockSpec((1, tok, HD), lambda h, *_: (part, 0, h)),
                head_spec(BLOCK),
                head_spec(BLOCK),
            ]
            + more_specs,
            out_specs=[head_spec(x.shape[0]) for x in outs],
            scratch_shapes=[pltpu.VMEM((HEADS * per_dev, BLOCK, HD), jnp.float32)],
        ),
        out_shape=outs,
        compiler_params=VMEM,
        name=name,
    )(place, served, *inputs, *more)


def shards(queries, keys, values, key_gain, random_blocks, out_grad):
    tok = queries.shape[1]
    width = queries.shape[2]
    per_dev = tok // BLOCK
    owners = lax.axis_size("seq")
    seq_place = lax.axis_index("seq")
    first_block = seq_place * per_dev
    place = jnp.stack([first_block, jnp.int32(owners * per_dev)]).astype(jnp.int32)
    q, v, g = queries[0], values[0], out_grad[0]
    key_eff = (keys[0].astype(jnp.float32) * key_gain).astype(jnp.bfloat16)

    request_count = HEADS * per_dev * NR
    capacity = (request_count + owners - 1) // owners + 3
    target = random_blocks.reshape(request_count)
    owner_dev = target // per_dev
    table_index = (
        jnp.arange(request_count, dtype=jnp.int32) // (per_dev * NR) * per_dev + target % per_dev
    )
    onehot = (owner_dev[:, None] == jnp.arange(owners, dtype=jnp.int32)[None, :]).astype(jnp.int32)
    before = jnp.cumsum(onehot, axis=0) - onehot
    slot_rank = jnp.sum(before * onehot, axis=1)
    position = (owner_dev * capacity + slot_rank).astype(jnp.int32)
    hit = position[:, None] == jnp.arange(owners * capacity, dtype=jnp.int32)[None, :]
    outgoing = (
        jnp.sum(jnp.where(hit, table_index[:, None] + 1, 0), axis=0).astype(jnp.int32) - 1
    ).reshape(owners, capacity)
    served = lax.all_to_all(outgoing, "seq", split_axis=0, concat_axis=0, tiled=True)
    served = served.reshape(owners * capacity)
    picked_k, picked_v = pick(served, key_eff, v, per_dev)

    def exchange(slots, *extra):
        parts = [slots.reshape(owners, capacity, BLOCK, HD)]
        for rows in extra:
            parts.append(rows.astype(jnp.bfloat16).reshape(owners, -1, BLOCK, HD))
        shaped = jnp.concatenate(parts, axis=1) if extra else parts[0]
        return lax.all_to_all(shaped, "seq", split_axis=0, concat_axis=0, tiled=True)

    def fetch(slots):
        return exchange(slots).reshape(owners * capacity, BLOCK, HD)

    def to_all(array):
        spread = jnp.broadcast_to(array[None], (owners,) + array.shape)
        return lax.all_to_all(spread, "seq", split_axis=0, concat_axis=0, tiled=True)

    edge = jnp.stack([q[:EDGE], key_eff[:EDGE], v[:EDGE], g[:EDGE]])
    edge = spread(edge.reshape(16, 4 * EDGE // 16, width), owners).reshape(4, EDGE, width)
    picked_k, edge = lax.optimization_barrier((picked_k, edge))
    tails = jnp.stack([key_eff[tok - BLOCK :], v[tok - BLOCK :]])
    heads = jnp.stack([key_eff[:BLOCK], v[:BLOCK]])
    left = passed_along(tails, "seq", 1)
    right = passed_along(heads, "seq", -1)
    arrived_k = fetch(picked_k)

    stat = (HEADS, 1, EDGE)
    edge_in = head_spec_3(4, EDGE)
    top, total, numer = edge_call(
        edge_sum_kernel,
        (edge, key_eff, v),
        [edge_in, head_spec(tok), head_spec(tok)],
        [stat, stat, (EDGE, width)],
        [row_spec(), row_spec(), head_spec(EDGE)],
        "sums",
    )
    share = EDGE // owners
    stats = jnp.concatenate([top[:, 0].T, total[:, 0].T], axis=1)
    stats = jnp.pad(stats, ((0, 0), (0, HD - 2 * HEADS)))
    parts = jnp.concatenate([numer, stats], axis=1).reshape(owners, share, width + HD)

    picked_v, arrived_k, parts = lax.optimization_barrier((picked_v, arrived_k, parts))
    arrived_v = fetch(picked_v)
    base = [q, g, key_eff, left, right, edge, arrived_k]
    value_global, value_padded, send_v = sparse(
        value_kernel, place, position, base, [], per_dev, 0, "value_terms"
    )

    parts = lax.all_to_all(parts, "seq", split_axis=0, concat_axis=0, tiled=True)
    tops = parts[:, :, width : width + HEADS]
    top_row = jnp.max(tops, axis=0)
    factor = jnp.exp(tops - top_row[None])
    total_row = jnp.sum(factor * parts[:, :, width + HEADS : width + 2 * HEADS], axis=0)
    numer_row = jnp.sum(
        parts[:, :, :width].reshape(owners, share, HEADS, HD) * factor[..., None], axis=0
    )
    out_row = (numer_row / total_row[..., None]).astype(jnp.bfloat16)
    grad_row = lax.dynamic_slice_in_dim(edge[3], seq_place * share, share, axis=0)
    grad_row = grad_row.reshape(share, HEADS, HD).astype(jnp.float32)
    delta_row = jnp.sum(grad_row * out_row.astype(jnp.float32), axis=2)
    row_stats = to_all(jnp.concatenate([top_row, total_row, delta_row], axis=1))
    row_stats = row_stats.reshape(EDGE, 3, HEADS).transpose(1, 2, 0)[:, :, None]

    arrived_v, send_v, row_stats = lax.optimization_barrier((arrived_v, send_v, row_stats))
    returned_v = exchange(send_v, value_global)
    key_global, key_padded, send_k, att, dq = sparse(
        key_kernel, place, position, base, [v, arrived_v], per_dev, 2, "key_terms"
    )
    edge_dq, local = edge_call(
        edge_grad_kernel,
        (edge, key_eff, v, row_stats[0], row_stats[1], row_stats[2]),
        [edge_in, head_spec(tok), head_spec(tok), row_spec(), row_spec(), row_spec()],
        [(EDGE, width), (2, tok, width)],
        [head_spec(EDGE), head_spec_3(2, tok)],
        "grads",
    )

    def neighbours(padded):
        nxt = passed_along(padded[:BLOCK].astype(jnp.bfloat16), "seq", -1)
        prev = passed_along(padded[tok + BLOCK :].astype(jnp.bfloat16), "seq", 1)
        return nxt, prev

    near_v = neighbours(value_padded)
    near_k = neighbours(key_padded)
    send_k, edge_dq, returned_v = lax.optimization_barrier((send_k, edge_dq, returned_v))
    returned_k = exchange(send_k, key_global, edge_dq)
    (dv,) = final(
        final_value_kernel, 1, capacity, place, served,
        (returned_v, value_padded, local, *near_v), (), per_dev, "final_value",
    )
    returned_k, dv = lax.optimization_barrier((returned_k, dv))

    def summed(block):
        return jnp.sum(block.astype(jnp.float32), axis=0).astype(jnp.bfloat16).reshape(share, width)

    piece = jnp.concatenate(
        [
            summed(returned_k[:, capacity]),
            summed(returned_v[:, capacity]),
            summed(returned_k[:, capacity + 1]),
            out_row.reshape(share, width),
        ]
    )
    collected = collect(piece, owners).reshape(owners, 4, share, width)
    collected = collected.transpose(1, 0, 2, 3).reshape(4, EDGE, width)
    dk, att, dq, dv, gain_term = final(
        final_key_kernel, 0, capacity, place, served,
        (returned_k, key_padded, local, *near_k),
        (
            collected[0], collected[1], collected[2], collected[3], keys[0], key_gain[None], att,
            dq, dv,
        ),
        per_dev, "final_key",
    )
    gain_grad = lax.psum(jnp.sum(to_all(gain_term), axis=(0, 1)), "dp")
    return att[None], dq[None], dk[None], dv[None], gain_grad


def solution(mesh):
    placed = (
        P("dp", "seq", None),
        P("dp", "seq", None),
        P("dp", "seq", None),
        P(),
        P(None, "seq", None),
        P("dp", "seq", None),
    )
    return jax.shard_map(
        shards,
        mesh=mesh,
        in_specs=placed,
        out_specs=(
            P("dp", "seq", None),
            P("dp", "seq", None),
            P("dp", "seq", None),
            P("dp", "seq", None),
            P(),
        ),
        check_vma=False,
    )
```

```python
import functools

import jax
import jax.numpy as jnp
from jax import lax
from jax.experimental import pallas as pl
from jax.experimental.pallas import tpu as pltpu
from jax.sharding import PartitionSpec as P

HEADS = 16
HD = 128
BLOCK = 64
NG = 2
NR = 3
NK = 8
EDGE = NG * BLOCK
SCALE = HD ** (-0.5)
NEGATIVE = -1e30
VMEM = pltpu.CompilerParams(vmem_limit_bytes=56 * 1024 * 1024)
WHOLE = pl.BlockSpec(memory_space=pltpu.VMEM)


def dot_nt(a, b):
    return lax.dot_general(a, b, (((1,), (1,)), ((), ())), preferred_element_type=jnp.float32)


def dot_nn(a, b):
    return lax.dot_general(a, b, (((1,), (0,)), ((), ())), preferred_element_type=jnp.float32)


def dot_tn(a, b):
    return lax.dot_general(a, b, (((0,), (0,)), ((), ())), preferred_element_type=jnp.float32)


def passed_along(array, axis, by):
    length = lax.axis_size(axis)
    pairs = [(i, i + by) for i in range(length) if 0 <= i + by < length]
    return lax.ppermute(array, axis, pairs)


def on(device):
    return dict(device_id={"seq": device}, device_id_type=pl.DeviceIdType.MESH)


def spread_kernel(count, in_ref, out_ref, send_sem, recv_sem):
    me = lax.axis_index("seq")
    children = (
        ((lax.rem(me, 8) == 0) & (me + 8 < count), 8),
        (lax.rem(me, 8) == 0, 4),
        (lax.rem(me, 4) == 0, 2),
        (lax.rem(me, 2) == 0, 1),
    )
    near = jnp.where(lax.rem(me, 4) == 2, me - 2, jnp.where(lax.rem(me, 8) == 4, me - 4, me - 8))
    parent = jnp.where(lax.rem(me, 2) == 1, me - 1, near)
    barrier = pltpu.get_barrier_semaphore()
    greeted = jnp.where(me > 0, 1, 0)
    for there, step in children:
        greeted = greeted + jnp.where(there, 1, 0)

        @pl.when(there)
        def _():
            pl.semaphore_signal(barrier, inc=1, **on(me + step))

    @pl.when(me > 0)
    def _():
        pl.semaphore_signal(barrier, inc=1, **on(parent))

    pl.semaphore_wait(barrier, greeted)

    @pl.when(me == 0)
    def _():
        out_ref[...] = in_ref[...]

    def copy(c, i, device):
        return pltpu.make_async_remote_copy(
            src_ref=out_ref.at[c],
            dst_ref=out_ref.at[c],
            send_sem=send_sem.at[i, c],
            recv_sem=recv_sem.at[c],
            **on(device),
        )

    def forward(c, carry):
        @pl.when(me > 0)
        def _():
            copy(c, 0, parent).wait_recv()

        for i, (there, step) in enumerate(children):

            @pl.when(there)
            def _():
                copy(c, i, me + step).start()

        return carry

    def finish(c, carry):
        for i, (there, step) in enumerate(children):

            @pl.when(there)
            def _():
                copy(c, i, me + step).wait_send()

        return carry

    lax.fori_loop(0, out_ref.shape[0], forward, 0)
    lax.fori_loop(0, out_ref.shape[0], finish, 0)


def spread(array, count):
    chunks = array.shape[0]
    return pl.pallas_call(
        functools.partial(spread_kernel, count),
        in_specs=[WHOLE],
        out_specs=WHOLE,
        out_shape=jax.ShapeDtypeStruct(array.shape, array.dtype),
        scratch_shapes=[
            pltpu.SemaphoreType.DMA((4, chunks)),
            pltpu.SemaphoreType.DMA((chunks,)),
        ],
        compiler_params=pltpu.CompilerParams(
            collective_id=0, has_side_effects=True, vmem_limit_bytes=32 * 1024 * 1024
        ),
        name="spread",
    )(array)


def collect_kernel(count, in_ref, out_ref, send_sem, recv_sem):
    me = lax.axis_index("seq")
    barrier = pltpu.get_barrier_semaphore()

    def copy(device):
        return pltpu.make_async_remote_copy(
            src_ref=in_ref,
            dst_ref=out_ref.at[device],
            send_sem=send_sem,
            recv_sem=recv_sem.at[device],
            **on(0),
        )

    @pl.when(me == 0)
    def _():
        def greet(d, carry):
            pl.semaphore_signal(barrier, inc=1, **on(d))
            return carry

        lax.fori_loop(1, count, greet, 0)
        pl.semaphore_wait(barrier, count - 1)
        out_ref[0] = in_ref[...]

        def receive(d, carry):
            copy(d).wait_recv()
            return carry

        lax.fori_loop(1, count, receive, 0)

    @pl.when(me > 0)
    def _():
        pl.semaphore_signal(barrier, inc=1, **on(0))
        pl.semaphore_wait(barrier, 1)
        copy(me).start()
        copy(me).wait_send()


def collect(piece, count, number):
    return pl.pallas_call(
        functools.partial(collect_kernel, count),
        in_specs=[WHOLE],
        out_specs=WHOLE,
        out_shape=jax.ShapeDtypeStruct((count,) + piece.shape, piece.dtype),
        scratch_shapes=[pltpu.SemaphoreType.DMA, pltpu.SemaphoreType.DMA((count,))],
        compiler_params=pltpu.CompilerParams(
            collective_id=number, has_side_effects=True, vmem_limit_bytes=32 * 1024 * 1024
        ),
        name=f"collect_{number}",
    )(piece)


def slot_rows(slot, capacity):
    start = pl.multiple_of(lax.rem(slot, capacity) * BLOCK, BLOCK)
    return lax.div(slot, capacity), pl.ds(start, BLOCK)


def pick_kernel(
    per_dev, capacity, index_ref, key_ref, value_ref, extra_ref, key_out, value_out
):
    filled = capacity * BLOCK
    key_out[:, filled:, :] = extra_ref[...]
    value_out[:, filled:, :] = jnp.zeros_like(value_out[:, filled:, :])

    def step(s, carry):
        table = jnp.maximum(index_ref[s], 0)
        rows = pl.ds(pl.multiple_of(lax.rem(table, per_dev) * BLOCK, BLOCK), BLOCK)
        cols = pl.ds(pl.multiple_of(lax.div(table, per_dev) * HD, HD), HD)
        owner, place = slot_rows(s, capacity)
        key_out[owner, place, :] = key_ref[rows, cols]
        value_out[owner, place, :] = value_ref[rows, cols]
        return carry

    lax.fori_loop(0, key_out.shape[0] * capacity, step, 0)


def pick(index, key_eff, values, extra, more, per_dev, capacity):
    owners = extra.shape[0]
    filled = capacity * BLOCK
    return pl.pallas_call(
        functools.partial(pick_kernel, per_dev, capacity),
        grid_spec=pltpu.PrefetchScalarGridSpec(
            num_scalar_prefetch=1, grid=(), in_specs=[WHOLE] * 3, out_specs=[WHOLE, WHOLE]
        ),
        out_shape=[
            jax.ShapeDtypeStruct((owners, filled + extra.shape[1], HD), jnp.bfloat16),
            jax.ShapeDtypeStruct((owners, filled + more, HD), jnp.bfloat16),
        ],
        compiler_params=VMEM,
        name="pick",
    )(index, key_eff, values, extra)


def in_parts(x):
    high = lax.reduce_precision(x, 8, 7)
    middle = lax.reduce_precision(x - high, 8, 7)
    return jnp.stack([high, middle, x - high - middle]).astype(jnp.bfloat16)


def from_parts(parts, axis):
    parts = parts.astype(jnp.float32)
    low = [lax.index_in_dim(parts, i, axis, keepdims=False) for i in range(3)]
    return low[0] + (low[1] + low[2])


def listed_rows(edge_rows, window_rows, p, arrived_ref, slots):
    window = window_rows[p * BLOCK : (p + 3) * BLOCK]
    return jnp.concatenate([edge_rows, window] + [arrived_ref[s[0], s[1], :] for s in slots], axis=0)


def softmax_parts(q, keys, block, total_blocks):
    column = lax.broadcasted_iota(jnp.int32, (1, NK * BLOCK), 1)
    listed = block - 1 - NG + column // BLOCK
    mask = (column < EDGE) | (column >= EDGE + 3 * BLOCK)
    mask = mask | ((listed >= NG) & (listed < total_blocks))
    scores = jnp.where(mask, dot_nt(q, keys) * SCALE, NEGATIVE)
    top = jnp.max(scores, axis=1, keepdims=True)
    expo = jnp.where(mask, jnp.exp(scores - top), 0.0)
    total = jnp.sum(expo, axis=1, keepdims=True)
    keep = jnp.where(block >= NG, 1.0, 0.0).astype(jnp.float32)
    return expo, total, expo * (keep / total)


def scatter_terms(terms, p, slots, global_ref, padded_ref, send_ref):
    global_ref[...] += terms[:EDGE]
    padded_ref[p * BLOCK : (p + 3) * BLOCK, :] += terms[EDGE : EDGE + 3 * BLOCK]
    for r in range(NR):
        start = EDGE + (3 + r) * BLOCK
        send_ref[slots[r][0], slots[r][1], :] = terms[start : start + BLOCK].astype(jnp.bfloat16)


def clear(head, global_ref, padded_ref, send_ref):
    @pl.when(head == 0)
    def _():
        send_ref[...] = jnp.zeros_like(send_ref)

    global_ref[...] = jnp.zeros_like(global_ref)
    padded_ref[...] = jnp.zeros_like(padded_ref)


def value_kernel(
    per_dev, capacity, place_ref, pos_ref, q_ref, g_ref, k_ref, left_ref, right_ref, edge_ref,
    arrived_ref, global_ref, padded_ref, send_ref,
):
    head = pl.program_id(0)
    clear(head, global_ref, padded_ref, send_ref)
    k_window = jnp.concatenate([left_ref[0], k_ref[...], right_ref[0]], axis=0)
    for p in range(per_dev):
        rows = slice(p * BLOCK, (p + 1) * BLOCK)
        slots = [
            slot_rows(pos_ref[(head * per_dev + p) * NR + r], capacity) for r in range(NR)
        ]
        keys = listed_rows(edge_ref[1], k_window, p, arrived_ref, slots)
        _, _, weights = softmax_parts(q_ref[rows, :], keys, place_ref[0] + p, place_ref[1])
        terms = dot_tn(weights.astype(jnp.bfloat16), g_ref[rows, :])
        scatter_terms(terms, p, slots, global_ref, padded_ref, send_ref)


def key_kernel(
    per_dev, capacity, place_ref, pos_ref, q_ref, g_ref, k_ref, left_ref, right_ref, edge_ref,
    arrived_ref, v_ref, arrived_v_ref, global_ref, padded_ref, send_ref, att_ref, dq_ref,
):
    head = pl.program_id(0)
    clear(head, global_ref, padded_ref, send_ref)
    k_window = jnp.concatenate([left_ref[0], k_ref[...], right_ref[0]], axis=0)
    v_window = jnp.concatenate([left_ref[1], v_ref[...], right_ref[1]], axis=0)
    for p in range(per_dev):
        rows = slice(p * BLOCK, (p + 1) * BLOCK)
        slots = [
            slot_rows(pos_ref[(head * per_dev + p) * NR + r], capacity) for r in range(NR)
        ]
        keys = listed_rows(edge_ref[1], k_window, p, arrived_ref, slots)
        values = listed_rows(edge_ref[2], v_window, p, arrived_v_ref, slots)
        q = q_ref[rows, :]
        g = g_ref[rows, :]
        expo, total, weights = softmax_parts(q, keys, place_ref[0] + p, place_ref[1])
        attended = (dot_nn(expo.astype(jnp.bfloat16), values) / total).astype(jnp.bfloat16)
        delta = jnp.sum(
            g.astype(jnp.float32) * attended.astype(jnp.float32), axis=1, keepdims=True
        )
        dscores = (weights * (dot_nt(g, values) - delta) * SCALE).astype(jnp.bfloat16)
        att_ref[rows, :] = attended
        dq_ref[rows, :] = dot_nn(dscores, keys).astype(jnp.bfloat16)
        scatter_terms(dot_tn(dscores, q), p, slots, global_ref, padded_ref, send_ref)


def head_spec(rows):
    return pl.BlockSpec((rows, HD), lambda h, *_: (0, h))


def head_spec_3(parts, rows):
    return pl.BlockSpec((parts, rows, HD), lambda h, *_: (0, 0, h))


def row_spec():
    return pl.BlockSpec((1, 1, EDGE), lambda h, *_: (h, 0, 0))


def sparse(kernel, place, position, inputs, more, per_dev, capacity, extra, outs, name):
    q = inputs[0]
    tok = q.shape[0]
    width = q.shape[1]
    wide = tok + 2 * BLOCK
    slots = (inputs[6].shape[0], capacity * BLOCK + extra, HD)
    return pl.pallas_call(
        functools.partial(kernel, per_dev, capacity),
        grid_spec=pltpu.PrefetchScalarGridSpec(
            num_scalar_prefetch=2,
            grid=(HEADS,),
            in_specs=[head_spec(tok)] * 3
            + [head_spec_3(2, BLOCK)] * 2
            + [head_spec_3(4, EDGE), WHOLE]
            + [head_spec(tok), WHOLE][: len(more)],
            out_specs=[head_spec(EDGE), head_spec(wide), WHOLE] + [head_spec(tok)] * outs,
        ),
        out_shape=[
            jax.ShapeDtypeStruct((EDGE, width), jnp.float32),
            jax.ShapeDtypeStruct((wide, width), jnp.float32),
            jax.ShapeDtypeStruct(slots, jnp.bfloat16),
        ]
        + [jax.ShapeDtypeStruct((tok, width), jnp.bfloat16)] * outs,
        compiler_params=VMEM,
        name=name,
    )(place, position, *inputs, *more)


def edge_sum_kernel(edge_ref, k_ref, v_ref, top_ref, total_ref, numer_ref):
    scores = dot_nt(k_ref[...], edge_ref[0]) * SCALE
    top = jnp.max(scores, axis=0, keepdims=True)
    expo = jnp.exp(scores - top)
    top_ref[0] = top
    total_ref[0] = jnp.sum(expo, axis=0, keepdims=True)
    numer_ref[...] = dot_tn(expo.astype(jnp.bfloat16), v_ref[...])


def edge_grad_kernel(edge_ref, k_ref, v_ref, top_ref, total_ref, delta_ref, dq_ref, dkv_ref):
    q = edge_ref[0]
    g = edge_ref[3]
    scores = dot_nt(k_ref[...], q) * SCALE
    weights = jnp.exp(scores - top_ref[0]) / total_ref[0]
    dprobs = dot_nt(v_ref[...], g)
    dscores = (weights * (dprobs - delta_ref[0]) * SCALE).astype(jnp.bfloat16)
    dq_ref[...] = dot_tn(dscores, k_ref[...])
    dkv_ref[0] = dot_nn(dscores, q)
    dkv_ref[1] = dot_nn(weights.astype(jnp.bfloat16), g)


def edge_call(kernel, inputs, specs, outs, out_specs, name):
    return pl.pallas_call(
        kernel,
        grid=(HEADS,),
        in_specs=specs,
        out_specs=out_specs,
        out_shape=[jax.ShapeDtypeStruct(s, jnp.float32) for s in outs],
        compiler_params=VMEM,
        name=name,
    )(*inputs)


def sum_terms(
    per_dev, capacity, place_ref, served_ref, returned_ref, padded_ref, local_ref, next_ref,
    prev_ref, global_ref, acc_ref,
):
    head = pl.program_id(0)

    @pl.when(head == 0)
    def _():
        acc_ref[...] = jnp.zeros_like(acc_ref)

        def step(s, carry):
            table = served_ref[s]

            @pl.when(table >= 0)
            def _():
                owner, rows = slot_rows(s, capacity)
                acc_ref[table] += returned_ref[owner, rows, :].astype(jnp.float32)

            return carry

        lax.fori_loop(0, returned_ref.shape[0] * capacity, step, 0)

    sums = []
    for p in range(per_dev):
        rows = slice(p * BLOCK, (p + 1) * BLOCK)
        shifted = slice((p + 1) * BLOCK, (p + 2) * BLOCK)
        term = padded_ref[shifted, :] + local_ref[0, rows, :] + acc_ref[head * per_dev + p]
        if p == per_dev - 1:
            term = term + next_ref[...].astype(jnp.float32)
        if p == 0:
            term = term + prev_ref[...].astype(jnp.float32)
        if global_ref is not None and p < NG:
            whole = global_ref[rows, :].astype(jnp.float32)
            term = term + jnp.where(place_ref[0] == 0, whole, 0.0)
        sums.append(term)
    return sums


def final_value_kernel(
    per_dev, capacity, place_ref, served_ref, returned_ref, padded_ref, local_ref, next_ref,
    prev_ref, dv_out, acc_ref,
):
    sums = sum_terms(
        per_dev, capacity, place_ref, served_ref, returned_ref, padded_ref, local_ref, next_ref,
        prev_ref, None, acc_ref,
    )
    for p in range(per_dev):
        dv_out[p * BLOCK : (p + 1) * BLOCK, :] = sums[p]


def final_key_kernel(
    per_dev, capacity, place_ref, served_ref, returned_ref, padded_ref, local_ref, next_ref,
    prev_ref, gk_ref, gv_ref, edq_ref, eout_ref, keys_ref, gain_ref, att_ref, dq_ref, dv_ref,
    dk_out, att_out, dq_out, dv_out, gain_out, acc_ref,
):
    sums = sum_terms(
        per_dev, capacity, place_ref, served_ref, returned_ref, padded_ref, local_ref, next_ref,
        prev_ref, gk_ref, acc_ref,
    )
    is_edge = place_ref[0] == 0
    gain_sum = jnp.zeros((1, HD), jnp.float32)
    for p in range(per_dev):
        rows = slice(p * BLOCK, (p + 1) * BLOCK)
        dk_out[rows, :] = (sums[p] * gain_ref[...]).astype(jnp.bfloat16)
        gain_sum = gain_sum + jnp.sum(
            sums[p] * keys_ref[rows, :].astype(jnp.float32), axis=0, keepdims=True
        )
        if p < NG:
            att_out[rows, :] = jnp.where(is_edge, eout_ref[rows, :], att_ref[rows, :])
            dq_out[rows, :] = jnp.where(is_edge, edq_ref[rows, :], dq_ref[rows, :])
            whole = jnp.where(is_edge, gv_ref[rows, :].astype(jnp.float32), 0.0)
            dv_out[rows, :] = (dv_ref[rows, :] + whole).astype(jnp.bfloat16)
        else:
            dv_out[rows, :] = dv_ref[rows, :].astype(jnp.bfloat16)
            att_out[rows, :] = att_ref[rows, :]
            dq_out[rows, :] = dq_ref[rows, :]
    gain_out[...] = gain_sum


def final(kernel, part, capacity, place, served, inputs, more, per_dev, name):
    tok = inputs[2].shape[1]
    width = inputs[2].shape[2]
    more_specs = [head_spec(x.shape[0]) for x in more]
    outs = [jax.ShapeDtypeStruct((tok, width), jnp.float32)]
    if more:
        outs = [jax.ShapeDtypeStruct((tok, width), jnp.bfloat16)] * 4
        outs = outs + [jax.ShapeDtypeStruct((1, width), jnp.float32)]
    return pl.pallas_call(
        functools.partial(kernel, per_dev, capacity),
        grid_spec=pltpu.PrefetchScalarGridSpec(
            num_scalar_prefetch=2,
            grid=(HEADS,),
            in_specs=[
                WHOLE,
                head_spec(tok + 2 * BLOCK),
                pl.BlockSpec((1, tok, HD), lambda h, *_: (part, 0, h)),
                head_spec(BLOCK),
                head_spec(BLOCK),
            ]
            + more_specs,
            out_specs=[head_spec(x.shape[0]) for x in outs],
            scratch_shapes=[pltpu.VMEM((HEADS * per_dev, BLOCK, HD), jnp.float32)],
        ),
        out_shape=outs,
        compiler_params=VMEM,
        name=name,
    )(place, served, *inputs, *more)


def shards(queries, keys, values, key_gain, random_blocks, out_grad):
    tok = queries.shape[1]
    width = queries.shape[2]
    per_dev = tok // BLOCK
    owners = lax.axis_size("seq")
    seq_place = lax.axis_index("seq")
    first_block = seq_place * per_dev
    place = jnp.stack([first_block, jnp.int32(owners * per_dev)]).astype(jnp.int32)
    q, v, g = queries[0], values[0], out_grad[0]
    key_eff = (keys[0].astype(jnp.float32) * key_gain).astype(jnp.bfloat16)

    request_count = HEADS * per_dev * NR
    capacity = (request_count + owners - 1) // owners + 3
    target = random_blocks.reshape(request_count)
    owner_dev = target // per_dev
    table_index = (
        jnp.arange(request_count, dtype=jnp.int32) // (per_dev * NR) * per_dev + target % per_dev
    )
    onehot = (owner_dev[:, None] == jnp.arange(owners, dtype=jnp.int32)[None, :]).astype(jnp.int32)
    before = jnp.cumsum(onehot, axis=0) - onehot
    slot_rank = jnp.sum(before * onehot, axis=1)
    position = (owner_dev * capacity + slot_rank).astype(jnp.int32)
    hit = position[:, None] == jnp.arange(owners * capacity, dtype=jnp.int32)[None, :]
    outgoing = (
        jnp.sum(jnp.where(hit, table_index[:, None] + 1, 0), axis=0).astype(jnp.int32) - 1
    ).reshape(owners, capacity)
    served = lax.all_to_all(outgoing, "seq", split_axis=0, concat_axis=0, tiled=True)
    served = served.reshape(owners * capacity)
    filled = capacity * BLOCK

    def exchange(slots):
        return lax.all_to_all(slots, "seq", split_axis=0, concat_axis=0, tiled=True)

    def to_all(array):
        spread_out = jnp.broadcast_to(array[None], (owners,) + array.shape)
        return lax.all_to_all(spread_out, "seq", split_axis=0, concat_axis=0, tiled=True)

    def pieces(rows):
        return rows.astype(jnp.bfloat16).reshape(owners, -1, HD)

    def padded_rows(flat, count):
        flat = jnp.pad(flat, ((0, 0), (0, count * HD - flat.shape[1])))
        return flat.reshape(flat.shape[0], count, HD)

    edge = jnp.stack([q[:EDGE], key_eff[:EDGE], v[:EDGE], g[:EDGE]])
    edge = spread(edge.reshape(16, 4 * EDGE // 16, width), owners).reshape(4, EDGE, width)
    tails = jnp.stack([key_eff[tok - BLOCK :], v[tok - BLOCK :]])
    heads = jnp.stack([key_eff[:BLOCK], v[:BLOCK]])
    left = passed_along(tails, "seq", 1)
    right = passed_along(heads, "seq", -1)

    stat = (HEADS, 1, EDGE)
    edge_in = head_spec_3(4, EDGE)
    top, total, numer = edge_call(
        edge_sum_kernel,
        (edge, key_eff, v),
        [edge_in, head_spec(tok), head_spec(tok)],
        [stat, stat, (EDGE, width)],
        [row_spec(), row_spec(), head_spec(EDGE)],
        "sums",
    )
    share = EDGE // owners
    stats = in_parts(jnp.concatenate([top[:, 0], total[:, 0]])).transpose(2, 0, 1)
    stats = padded_rows(stats.reshape(owners, share * 6 * HEADS), 16)
    extra = jnp.concatenate([pieces(numer), stats], axis=1)
    picked_k, picked_v = pick(served, key_eff, v, extra, 16, per_dev, capacity)
    picked_k, left, right = lax.optimization_barrier((picked_k, left, right))
    arrived_k = exchange(picked_k)
    parts = arrived_k[:, filled : filled + share * width // HD]
    parts = parts.reshape(owners, share, HEADS, HD).astype(jnp.float32)
    stats = arrived_k[:, filled + share * width // HD :].reshape(owners, -1)
    stats = stats[:, : share * 6 * HEADS].reshape(owners, share, 3, 2 * HEADS)
    stats = from_parts(stats, 2)
    tops = stats[:, :, :HEADS]
    top_row = jnp.max(tops, axis=0)
    factor = jnp.exp(tops - top_row[None])
    total_row = jnp.sum(factor * stats[:, :, HEADS:], axis=0)
    numer_row = jnp.sum(parts * factor[..., None], axis=0)
    out_row = (numer_row / total_row[..., None]).astype(jnp.bfloat16)
    grad_row = lax.dynamic_slice_in_dim(edge[3], seq_place * share, share, axis=0)
    grad_row = grad_row.reshape(share, HEADS, HD).astype(jnp.float32)
    delta_row = jnp.sum(grad_row * out_row.astype(jnp.float32), axis=2)
    row_stats = in_parts(jnp.stack([top_row, total_row, delta_row]))
    row_stats = padded_rows(row_stats.reshape(1, 9 * share * HEADS), 16)
    picked_v = picked_v.at[:, filled:].set(jnp.broadcast_to(row_stats, (owners, 16, HD)))
    arrived_v = exchange(picked_v)

    base = [q, g, key_eff, left, right, edge, arrived_k]
    value_global, value_padded, send_v = sparse(
        value_kernel, place, position, base, [], per_dev, capacity, share * width // HD, 0,
        "value_terms",
    )
    arrived_v, send_v, value_global = lax.optimization_barrier((arrived_v, send_v, value_global))
    row_stats = arrived_v[:, filled:].reshape(owners, -1)[:, : 9 * share * HEADS]
    row_stats = from_parts(row_stats.reshape(owners, 3, 3, share, HEADS), 1)
    row_stats = row_stats.transpose(1, 3, 0, 2).reshape(3, HEADS, 1, EDGE)
    returned_v = exchange(send_v.at[:, filled:].set(pieces(value_global)))
    key_global, key_padded, send_k, att, dq = sparse(
        key_kernel, place, position, base, [v, arrived_v], per_dev, capacity,
        2 * share * width // HD, 2, "key_terms",
    )
    edge_dq, local = edge_call(
        edge_grad_kernel,
        (edge, key_eff, v, row_stats[0], row_stats[1], row_stats[2]),
        [edge_in, head_spec(tok), head_spec(tok), row_spec(), row_spec(), row_spec()],
        [(EDGE, width), (2, tok, width)],
        [head_spec(EDGE), head_spec_3(2, tok)],
        "grads",
    )

    def neighbours(padded):
        nxt = passed_along(padded[:BLOCK].astype(jnp.bfloat16), "seq", -1)
        prev = passed_along(padded[tok + BLOCK :].astype(jnp.bfloat16), "seq", 1)
        return nxt, prev

    near_v = neighbours(value_padded)
    near_k = neighbours(key_padded)
    extra = jnp.concatenate([pieces(key_global), pieces(edge_dq)], axis=1)
    send_k = send_k.at[:, filled:].set(extra)
    send_k, returned_v = lax.optimization_barrier((send_k, returned_v))
    returned_k = exchange(send_k)
    (dv,) = final(
        final_value_kernel, 1, capacity, place, served,
        (returned_v, value_padded, local, *near_v), (), per_dev, "final_value",
    )

    def summed(block):
        return jnp.sum(block.astype(jnp.float32), axis=0).astype(jnp.bfloat16).reshape(share, width)

    def collected(first, second, number):
        got = collect(jnp.concatenate([first, second]).reshape(16, -1), owners, number)
        return got.reshape(owners, 2, share, width).transpose(1, 0, 2, 3).reshape(2, EDGE, width)

    global_v, edge_out = collected(summed(returned_v[:, filled:]), out_row.reshape(share, width), 1)
    returned_k, dv, global_v, edge_out = lax.optimization_barrier(
        (returned_k, dv, global_v, edge_out)
    )
    count = share * width // HD
    global_k, edge_dq = collected(
        summed(returned_k[:, filled : filled + count]), summed(returned_k[:, filled + count :]), 2
    )
    dk, att, dq, dv, gain_term = final(
        final_key_kernel, 0, capacity, place, served,
        (returned_k, key_padded, local, *near_k),
        (
            global_k, global_v, edge_dq, edge_out, keys[0], key_gain[None], att, dq, dv,
        ),
        per_dev, "final_key",
    )
    gain_grad = lax.psum(jnp.sum(to_all(gain_term), axis=(0, 1)), "dp")
    return att[None], dq[None], dk[None], dv[None], gain_grad


def solution(mesh):
    placed = (
        P("dp", "seq", None),
        P("dp", "seq", None),
        P("dp", "seq", None),
        P(),
        P(None, "seq", None),
        P("dp", "seq", None),
    )
    return jax.shard_map(
        shards,
        mesh=mesh,
        in_specs=placed,
        out_specs=(
            P("dp", "seq", None),
            P("dp", "seq", None),
            P("dp", "seq", None),
            P("dp", "seq", None),
            P(),
        ),
        check_vma=False,
    )
```

```python
import functools

import jax
import jax.numpy as jnp
from jax import lax
from jax.experimental import pallas as pl
from jax.experimental.pallas import tpu as pltpu
from jax.sharding import PartitionSpec as P

HEADS = 16
HD = 128
BLOCK = 64
NG = 2
NR = 3
NK = 8
EDGE = NG * BLOCK
SCALE = HD ** (-0.5)
NEGATIVE = -1e30
VMEM = pltpu.CompilerParams(vmem_limit_bytes=56 * 1024 * 1024)
WHOLE = pl.BlockSpec(memory_space=pltpu.VMEM)


def dot_nt(a, b):
    return lax.dot_general(a, b, (((1,), (1,)), ((), ())), preferred_element_type=jnp.float32)


def dot_nn(a, b):
    return lax.dot_general(a, b, (((1,), (0,)), ((), ())), preferred_element_type=jnp.float32)


def dot_tn(a, b):
    return lax.dot_general(a, b, (((0,), (0,)), ((), ())), preferred_element_type=jnp.float32)


def passed_along(array, axis, by):
    length = lax.axis_size(axis)
    pairs = [(i, i + by) for i in range(length) if 0 <= i + by < length]
    return lax.ppermute(array, axis, pairs)


def on(device):
    return dict(device_id={"seq": device}, device_id_type=pl.DeviceIdType.MESH)


def spread_kernel(count, in_ref, out_ref, send_sem, recv_sem):
    me = lax.axis_index("seq")
    children = (
        ((lax.rem(me, 8) == 0) & (me + 8 < count), 8),
        (lax.rem(me, 8) == 0, 4),
        (lax.rem(me, 4) == 0, 2),
        (lax.rem(me, 2) == 0, 1),
    )
    near = jnp.where(lax.rem(me, 4) == 2, me - 2, jnp.where(lax.rem(me, 8) == 4, me - 4, me - 8))
    parent = jnp.where(lax.rem(me, 2) == 1, me - 1, near)
    barrier = pltpu.get_barrier_semaphore()
    greeted = jnp.where(me > 0, 1, 0)
    for there, step in children:
        greeted = greeted + jnp.where(there, 1, 0)

        @pl.when(there)
        def _():
            pl.semaphore_signal(barrier, inc=1, **on(me + step))

    @pl.when(me > 0)
    def _():
        pl.semaphore_signal(barrier, inc=1, **on(parent))

    pl.semaphore_wait(barrier, greeted)

    @pl.when(me == 0)
    def _():
        out_ref[...] = in_ref[...]

    def copy(c, i, device):
        return pltpu.make_async_remote_copy(
            src_ref=out_ref.at[c],
            dst_ref=out_ref.at[c],
            send_sem=send_sem.at[i, c],
            recv_sem=recv_sem.at[c],
            **on(device),
        )

    def forward(c, carry):
        @pl.when(me > 0)
        def _():
            copy(c, 0, parent).wait_recv()

        for i, (there, step) in enumerate(children):

            @pl.when(there)
            def _():
                copy(c, i, me + step).start()

        return carry

    def finish(c, carry):
        for i, (there, step) in enumerate(children):

            @pl.when(there)
            def _():
                copy(c, i, me + step).wait_send()

        return carry

    lax.fori_loop(0, out_ref.shape[0], forward, 0)
    lax.fori_loop(0, out_ref.shape[0], finish, 0)


def spread(array, count):
    chunks = array.shape[0]
    return pl.pallas_call(
        functools.partial(spread_kernel, count),
        in_specs=[WHOLE],
        out_specs=WHOLE,
        out_shape=jax.ShapeDtypeStruct(array.shape, array.dtype),
        scratch_shapes=[
            pltpu.SemaphoreType.DMA((4, chunks)),
            pltpu.SemaphoreType.DMA((chunks,)),
        ],
        compiler_params=pltpu.CompilerParams(
            collective_id=0, has_side_effects=True, vmem_limit_bytes=32 * 1024 * 1024
        ),
        name="spread",
    )(array)


def collect_kernel(count, in_ref, out_ref, send_sem, recv_sem):
    me = lax.axis_index("seq")
    barrier = pltpu.get_barrier_semaphore()

    def copy(device):
        return pltpu.make_async_remote_copy(
            src_ref=in_ref,
            dst_ref=out_ref.at[device],
            send_sem=send_sem,
            recv_sem=recv_sem.at[device],
            **on(0),
        )

    @pl.when(me == 0)
    def _():
        def greet(d, carry):
            pl.semaphore_signal(barrier, inc=1, **on(d))
            return carry

        lax.fori_loop(1, count, greet, 0)
        pl.semaphore_wait(barrier, count - 1)
        out_ref[0] = in_ref[...]

        def receive(d, carry):
            copy(d).wait_recv()
            return carry

        lax.fori_loop(1, count, receive, 0)

    @pl.when(me > 0)
    def _():
        pl.semaphore_signal(barrier, inc=1, **on(0))
        pl.semaphore_wait(barrier, 1)
        copy(me).start()
        copy(me).wait_send()


def collect(piece, count, number):
    return pl.pallas_call(
        functools.partial(collect_kernel, count),
        in_specs=[WHOLE],
        out_specs=WHOLE,
        out_shape=jax.ShapeDtypeStruct((count,) + piece.shape, piece.dtype),
        scratch_shapes=[pltpu.SemaphoreType.DMA, pltpu.SemaphoreType.DMA((count,))],
        compiler_params=pltpu.CompilerParams(
            collective_id=number, has_side_effects=True, vmem_limit_bytes=32 * 1024 * 1024
        ),
        name=f"collect_{number}",
    )(piece)


def slot_rows(slot, capacity):
    start = pl.multiple_of(lax.rem(slot, capacity) * BLOCK, BLOCK)
    return lax.div(slot, capacity), pl.ds(start, BLOCK)


def pick_kernel(
    per_dev, capacity, index_ref, key_ref, value_ref, extra_ref, key_out, value_out
):
    filled = capacity * BLOCK
    key_out[:, filled:, :] = extra_ref[...]
    value_out[:, filled:, :] = jnp.zeros_like(value_out[:, filled:, :])

    def step(s, carry):
        table = jnp.maximum(index_ref[s], 0)
        rows = pl.ds(pl.multiple_of(lax.rem(table, per_dev) * BLOCK, BLOCK), BLOCK)
        cols = pl.ds(pl.multiple_of(lax.div(table, per_dev) * HD, HD), HD)
        owner, place = slot_rows(s, capacity)
        key_out[owner, place, :] = key_ref[rows, cols]
        value_out[owner, place, :] = value_ref[rows, cols]
        return carry

    lax.fori_loop(0, key_out.shape[0] * capacity, step, 0, unroll=4)


def pick(index, key_eff, values, extra, more, per_dev, capacity):
    owners = extra.shape[0]
    filled = capacity * BLOCK
    return pl.pallas_call(
        functools.partial(pick_kernel, per_dev, capacity),
        grid_spec=pltpu.PrefetchScalarGridSpec(
            num_scalar_prefetch=1, grid=(), in_specs=[WHOLE] * 3, out_specs=[WHOLE, WHOLE]
        ),
        out_shape=[
            jax.ShapeDtypeStruct((owners, filled + extra.shape[1], HD), jnp.bfloat16),
            jax.ShapeDtypeStruct((owners, filled + more, HD), jnp.bfloat16),
        ],
        compiler_params=VMEM,
        name="pick",
    )(index, key_eff, values, extra)


def in_parts(x):
    high = lax.reduce_precision(x, 8, 7)
    middle = lax.reduce_precision(x - high, 8, 7)
    return jnp.stack([high, middle, x - high - middle]).astype(jnp.bfloat16)


def from_parts(parts, axis):
    parts = parts.astype(jnp.float32)
    low = [lax.index_in_dim(parts, i, axis, keepdims=False) for i in range(3)]
    return low[0] + (low[1] + low[2])


def listed_rows(edge_rows, window_rows, p, arrived_ref, slots):
    window = window_rows[p * BLOCK : (p + 3) * BLOCK]
    return jnp.concatenate([edge_rows, window] + [arrived_ref[s[0], s[1], :] for s in slots], axis=0)


def softmax_parts(q, keys, block, total_blocks):
    column = lax.broadcasted_iota(jnp.int32, (1, NK * BLOCK), 1)
    listed = block - 1 - NG + column // BLOCK
    mask = (column < EDGE) | (column >= EDGE + 3 * BLOCK)
    mask = mask | ((listed >= NG) & (listed < total_blocks))
    scores = jnp.where(mask, dot_nt(q, keys) * SCALE, NEGATIVE)
    top = jnp.max(scores, axis=1, keepdims=True)
    expo = jnp.where(mask, jnp.exp(scores - top), 0.0)
    total = jnp.sum(expo, axis=1, keepdims=True)
    keep = jnp.where(block >= NG, 1.0, 0.0).astype(jnp.float32)
    return expo, total, expo * (keep / total)


def scatter_terms(terms, p, slots, global_ref, padded_ref, send_ref):
    global_ref[...] += terms[:EDGE]
    padded_ref[p * BLOCK : (p + 3) * BLOCK, :] += terms[EDGE : EDGE + 3 * BLOCK]
    for r in range(NR):
        start = EDGE + (3 + r) * BLOCK
        send_ref[slots[r][0], slots[r][1], :] = terms[start : start + BLOCK].astype(jnp.bfloat16)


def clear(head, global_ref, padded_ref, send_ref):
    @pl.when(head == 0)
    def _():
        send_ref[...] = jnp.zeros_like(send_ref)

    global_ref[...] = jnp.zeros_like(global_ref)
    padded_ref[...] = jnp.zeros_like(padded_ref)


def value_kernel(
    per_dev, capacity, place_ref, pos_ref, q_ref, g_ref, k_ref, left_ref, right_ref, edge_ref,
    arrived_ref, global_ref, padded_ref, send_ref,
):
    head = pl.program_id(0)
    clear(head, global_ref, padded_ref, send_ref)
    k_window = jnp.concatenate([left_ref[0], k_ref[...], right_ref[0]], axis=0)
    for p in range(per_dev):
        rows = slice(p * BLOCK, (p + 1) * BLOCK)
        slots = [
            slot_rows(pos_ref[(head * per_dev + p) * NR + r], capacity) for r in range(NR)
        ]
        keys = listed_rows(edge_ref[1], k_window, p, arrived_ref, slots)
        _, _, weights = softmax_parts(q_ref[rows, :], keys, place_ref[0] + p, place_ref[1])
        terms = dot_tn(weights.astype(jnp.bfloat16), g_ref[rows, :])
        scatter_terms(terms, p, slots, global_ref, padded_ref, send_ref)


def key_kernel(
    per_dev, capacity, place_ref, pos_ref, q_ref, g_ref, k_ref, left_ref, right_ref, edge_ref,
    arrived_ref, v_ref, arrived_v_ref, global_ref, padded_ref, send_ref, att_ref, dq_ref,
):
    head = pl.program_id(0)
    clear(head, global_ref, padded_ref, send_ref)
    k_window = jnp.concatenate([left_ref[0], k_ref[...], right_ref[0]], axis=0)
    v_window = jnp.concatenate([left_ref[1], v_ref[...], right_ref[1]], axis=0)
    for p in range(per_dev):
        rows = slice(p * BLOCK, (p + 1) * BLOCK)
        slots = [
            slot_rows(pos_ref[(head * per_dev + p) * NR + r], capacity) for r in range(NR)
        ]
        keys = listed_rows(edge_ref[1], k_window, p, arrived_ref, slots)
        values = listed_rows(edge_ref[2], v_window, p, arrived_v_ref, slots)
        q = q_ref[rows, :]
        g = g_ref[rows, :]
        expo, total, weights = softmax_parts(q, keys, place_ref[0] + p, place_ref[1])
        attended = (dot_nn(expo.astype(jnp.bfloat16), values) / total).astype(jnp.bfloat16)
        delta = jnp.sum(
            g.astype(jnp.float32) * attended.astype(jnp.float32), axis=1, keepdims=True
        )
        dscores = (weights * (dot_nt(g, values) - delta) * SCALE).astype(jnp.bfloat16)
        att_ref[rows, :] = attended
        dq_ref[rows, :] = dot_nn(dscores, keys).astype(jnp.bfloat16)
        scatter_terms(dot_tn(dscores, q), p, slots, global_ref, padded_ref, send_ref)


def head_spec(rows):
    return pl.BlockSpec((rows, HD), lambda h, *_: (0, h))


def head_spec_3(parts, rows):
    return pl.BlockSpec((parts, rows, HD), lambda h, *_: (0, 0, h))


def row_spec():
    return pl.BlockSpec((1, 1, EDGE), lambda h, *_: (h, 0, 0))


def sparse(kernel, place, position, inputs, more, per_dev, capacity, extra, outs, name):
    q = inputs[0]
    tok = q.shape[0]
    width = q.shape[1]
    wide = tok + 2 * BLOCK
    slots = (inputs[6].shape[0], capacity * BLOCK + extra, HD)
    return pl.pallas_call(
        functools.partial(kernel, per_dev, capacity),
        grid_spec=pltpu.PrefetchScalarGridSpec(
            num_scalar_prefetch=2,
            grid=(HEADS,),
            in_specs=[head_spec(tok)] * 3
            + [head_spec_3(2, BLOCK)] * 2
            + [head_spec_3(4, EDGE), WHOLE]
            + [head_spec(tok), WHOLE][: len(more)],
            out_specs=[head_spec(EDGE), head_spec(wide), WHOLE] + [head_spec(tok)] * outs,
        ),
        out_shape=[
            jax.ShapeDtypeStruct((EDGE, width), jnp.float32),
            jax.ShapeDtypeStruct((wide, width), jnp.float32),
            jax.ShapeDtypeStruct(slots, jnp.bfloat16),
        ]
        + [jax.ShapeDtypeStruct((tok, width), jnp.bfloat16)] * outs,
        compiler_params=VMEM,
        name=name,
    )(place, position, *inputs, *more)


def edge_sum_kernel(edge_ref, k_ref, v_ref, top_ref, total_ref, numer_ref):
    scores = dot_nt(k_ref[...], edge_ref[0]) * SCALE
    top = jnp.max(scores, axis=0, keepdims=True)
    expo = jnp.exp(scores - top)
    top_ref[0] = top
    total_ref[0] = jnp.sum(expo, axis=0, keepdims=True)
    numer_ref[...] = dot_tn(expo.astype(jnp.bfloat16), v_ref[...])


def edge_grad_kernel(edge_ref, k_ref, v_ref, top_ref, total_ref, delta_ref, dq_ref, dkv_ref):
    q = edge_ref[0]
    g = edge_ref[3]
    scores = dot_nt(k_ref[...], q) * SCALE
    weights = jnp.exp(scores - top_ref[0]) / total_ref[0]
    dprobs = dot_nt(v_ref[...], g)
    dscores = (weights * (dprobs - delta_ref[0]) * SCALE).astype(jnp.bfloat16)
    dq_ref[...] = dot_tn(dscores, k_ref[...])
    dkv_ref[0] = dot_nn(dscores, q)
    dkv_ref[1] = dot_nn(weights.astype(jnp.bfloat16), g)


def edge_call(kernel, inputs, specs, outs, out_specs, name):
    return pl.pallas_call(
        kernel,
        grid=(HEADS,),
        in_specs=specs,
        out_specs=out_specs,
        out_shape=[jax.ShapeDtypeStruct(s, jnp.float32) for s in outs],
        compiler_params=VMEM,
        name=name,
    )(*inputs)


def sum_terms(
    per_dev, capacity, place_ref, served_ref, returned_ref, padded_ref, local_ref, next_ref,
    prev_ref, global_ref, acc_ref,
):
    head = pl.program_id(0)

    @pl.when(head == 0)
    def _():
        acc_ref[...] = jnp.zeros_like(acc_ref)

        def step(s, carry):
            table = served_ref[s]

            @pl.when(table >= 0)
            def _():
                owner, rows = slot_rows(s, capacity)
                acc_ref[table] += returned_ref[owner, rows, :].astype(jnp.float32)

            return carry

        lax.fori_loop(0, returned_ref.shape[0] * capacity, step, 0)

    sums = []
    for p in range(per_dev):
        rows = slice(p * BLOCK, (p + 1) * BLOCK)
        shifted = slice((p + 1) * BLOCK, (p + 2) * BLOCK)
        term = padded_ref[shifted, :] + local_ref[0, rows, :] + acc_ref[head * per_dev + p]
        if p == per_dev - 1:
            term = term + next_ref[...].astype(jnp.float32)
        if p == 0:
            term = term + prev_ref[...].astype(jnp.float32)
        if global_ref is not None and p < NG:
            whole = global_ref[rows, :].astype(jnp.float32)
            term = term + jnp.where(place_ref[0] == 0, whole, 0.0)
        sums.append(term)
    return sums


def final_value_kernel(
    per_dev, capacity, place_ref, served_ref, returned_ref, padded_ref, local_ref, next_ref,
    prev_ref, dv_out, acc_ref,
):
    sums = sum_terms(
        per_dev, capacity, place_ref, served_ref, returned_ref, padded_ref, local_ref, next_ref,
        prev_ref, None, acc_ref,
    )
    for p in range(per_dev):
        dv_out[p * BLOCK : (p + 1) * BLOCK, :] = sums[p]


def final_key_kernel(
    per_dev, capacity, place_ref, served_ref, returned_ref, padded_ref, local_ref, next_ref,
    prev_ref, gk_ref, gv_ref, edq_ref, eout_ref, keys_ref, gain_ref, att_ref, dq_ref, dv_ref,
    dk_out, att_out, dq_out, dv_out, gain_out, acc_ref,
):
    sums = sum_terms(
        per_dev, capacity, place_ref, served_ref, returned_ref, padded_ref, local_ref, next_ref,
        prev_ref, gk_ref, acc_ref,
    )
    is_edge = place_ref[0] == 0
    gain_sum = jnp.zeros((1, HD), jnp.float32)
    for p in range(per_dev):
        rows = slice(p * BLOCK, (p + 1) * BLOCK)
        dk_out[rows, :] = (sums[p] * gain_ref[...]).astype(jnp.bfloat16)
        gain_sum = gain_sum + jnp.sum(
            sums[p] * keys_ref[rows, :].astype(jnp.float32), axis=0, keepdims=True
        )
        if p < NG:
            att_out[rows, :] = jnp.where(is_edge, eout_ref[rows, :], att_ref[rows, :])
            dq_out[rows, :] = jnp.where(is_edge, edq_ref[rows, :], dq_ref[rows, :])
            whole = jnp.where(is_edge, gv_ref[rows, :].astype(jnp.float32), 0.0)
            dv_out[rows, :] = (dv_ref[rows, :] + whole).astype(jnp.bfloat16)
        else:
            dv_out[rows, :] = dv_ref[rows, :].astype(jnp.bfloat16)
            att_out[rows, :] = att_ref[rows, :]
            dq_out[rows, :] = dq_ref[rows, :]
    gain_out[...] = gain_sum


def final(kernel, part, capacity, place, served, inputs, more, per_dev, name):
    tok = inputs[2].shape[1]
    width = inputs[2].shape[2]
    more_specs = [head_spec(x.shape[0]) for x in more]
    outs = [jax.ShapeDtypeStruct((tok, width), jnp.float32)]
    if more:
        outs = [jax.ShapeDtypeStruct((tok, width), jnp.bfloat16)] * 4
        outs = outs + [jax.ShapeDtypeStruct((1, width), jnp.float32)]
    return pl.pallas_call(
        functools.partial(kernel, per_dev, capacity),
        grid_spec=pltpu.PrefetchScalarGridSpec(
            num_scalar_prefetch=2,
            grid=(HEADS,),
            in_specs=[
                WHOLE,
                head_spec(tok + 2 * BLOCK),
                pl.BlockSpec((1, tok, HD), lambda h, *_: (part, 0, h)),
                head_spec(BLOCK),
                head_spec(BLOCK),
            ]
            + more_specs,
            out_specs=[head_spec(x.shape[0]) for x in outs],
            scratch_shapes=[pltpu.VMEM((HEADS * per_dev, BLOCK, HD), jnp.float32)],
        ),
        out_shape=outs,
        compiler_params=VMEM,
        name=name,
    )(place, served, *inputs, *more)


def shards(queries, keys, values, key_gain, random_blocks, out_grad):
    tok = queries.shape[1]
    width = queries.shape[2]
    per_dev = tok // BLOCK
    owners = lax.axis_size("seq")
    seq_place = lax.axis_index("seq")
    first_block = seq_place * per_dev
    place = jnp.stack([first_block, jnp.int32(owners * per_dev)]).astype(jnp.int32)
    q, v, g = queries[0], values[0], out_grad[0]
    key_eff = (keys[0].astype(jnp.float32) * key_gain).astype(jnp.bfloat16)

    request_count = HEADS * per_dev * NR
    capacity = (request_count + owners - 1) // owners + 3
    target = random_blocks.reshape(request_count)
    owner_dev = target // per_dev
    table_index = (
        jnp.arange(request_count, dtype=jnp.int32) // (per_dev * NR) * per_dev + target % per_dev
    )
    onehot = (owner_dev[:, None] == jnp.arange(owners, dtype=jnp.int32)[None, :]).astype(jnp.int32)
    before = jnp.cumsum(onehot, axis=0) - onehot
    slot_rank = jnp.sum(before * onehot, axis=1)
    position = (owner_dev * capacity + slot_rank).astype(jnp.int32)
    hit = position[:, None] == jnp.arange(owners * capacity, dtype=jnp.int32)[None, :]
    outgoing = (
        jnp.sum(jnp.where(hit, table_index[:, None] + 1, 0), axis=0).astype(jnp.int32) - 1
    ).reshape(owners, capacity)
    served = lax.all_to_all(outgoing, "seq", split_axis=0, concat_axis=0, tiled=True)
    served = served.reshape(owners * capacity)
    filled = capacity * BLOCK

    def exchange(slots):
        return lax.all_to_all(slots, "seq", split_axis=0, concat_axis=0, tiled=True)

    def to_all(array):
        spread_out = jnp.broadcast_to(array[None], (owners,) + array.shape)
        return lax.all_to_all(spread_out, "seq", split_axis=0, concat_axis=0, tiled=True)

    def pieces(rows):
        return rows.astype(jnp.bfloat16).reshape(owners, -1, HD)

    def padded_rows(flat, count):
        flat = jnp.pad(flat, ((0, 0), (0, count * HD - flat.shape[1])))
        return flat.reshape(flat.shape[0], count, HD)

    edge = jnp.stack([q[:EDGE], key_eff[:EDGE], v[:EDGE], g[:EDGE]])
    edge = spread(edge.reshape(32, 4 * EDGE // 32, width), owners).reshape(4, EDGE, width)
    tails = jnp.stack([key_eff[tok - BLOCK :], v[tok - BLOCK :]])
    heads = jnp.stack([key_eff[:BLOCK], v[:BLOCK]])
    left = passed_along(tails, "seq", 1)
    right = passed_along(heads, "seq", -1)

    stat = (HEADS, 1, EDGE)
    edge_in = head_spec_3(4, EDGE)
    top, total, numer = edge_call(
        edge_sum_kernel,
        (edge, key_eff, v),
        [edge_in, head_spec(tok), head_spec(tok)],
        [stat, stat, (EDGE, width)],
        [row_spec(), row_spec(), head_spec(EDGE)],
        "sums",
    )
    share = EDGE // owners
    stats = in_parts(jnp.concatenate([top[:, 0], total[:, 0]])).transpose(2, 0, 1)
    stats = padded_rows(stats.reshape(owners, share * 6 * HEADS), 16)
    extra = jnp.concatenate([pieces(numer), stats], axis=1)
    picked_k, picked_v = pick(served, key_eff, v, extra, 16, per_dev, capacity)
    picked_k, left, right = lax.optimization_barrier((picked_k, left, right))
    arrived_k = exchange(picked_k)
    parts = arrived_k[:, filled : filled + share * width // HD]
    parts = parts.reshape(owners, share, HEADS, HD).astype(jnp.float32)
    stats = arrived_k[:, filled + share * width // HD :].reshape(owners, -1)
    stats = stats[:, : share * 6 * HEADS].reshape(owners, share, 3, 2 * HEADS)
    stats = from_parts(stats, 2)
    tops = stats[:, :, :HEADS]
    top_row = jnp.max(tops, axis=0)
    factor = jnp.exp(tops - top_row[None])
    total_row = jnp.sum(factor * stats[:, :, HEADS:], axis=0)
    numer_row = jnp.sum(parts * factor[..., None], axis=0)
    out_row = (numer_row / total_row[..., None]).astype(jnp.bfloat16)
    grad_row = lax.dynamic_slice_in_dim(edge[3], seq_place * share, share, axis=0)
    grad_row = grad_row.reshape(share, HEADS, HD).astype(jnp.float32)
    delta_row = jnp.sum(grad_row * out_row.astype(jnp.float32), axis=2)
    row_stats = in_parts(jnp.stack([top_row, total_row, delta_row]))
    row_stats = padded_rows(row_stats.reshape(1, 9 * share * HEADS), 16)
    picked_v = picked_v.at[:, filled:].set(jnp.broadcast_to(row_stats, (owners, 16, HD)))
    arrived_v = exchange(picked_v)

    base = [q, g, key_eff, left, right, edge, arrived_k]
    value_global, value_padded, send_v = sparse(
        value_kernel, place, position, base, [], per_dev, capacity, share * width // HD, 0,
        "value_terms",
    )
    arrived_v, send_v, value_global = lax.optimization_barrier((arrived_v, send_v, value_global))
    row_stats = arrived_v[:, filled:].reshape(owners, -1)[:, : 9 * share * HEADS]
    row_stats = from_parts(row_stats.reshape(owners, 3, 3, share, HEADS), 1)
    row_stats = row_stats.transpose(1, 3, 0, 2).reshape(3, HEADS, 1, EDGE)
    returned_v = exchange(send_v.at[:, filled:].set(pieces(value_global)))
    key_global, key_padded, send_k, att, dq = sparse(
        key_kernel, place, position, base, [v, arrived_v], per_dev, capacity,
        2 * share * width // HD, 2, "key_terms",
    )
    edge_dq, local = edge_call(
        edge_grad_kernel,
        (edge, key_eff, v, row_stats[0], row_stats[1], row_stats[2]),
        [edge_in, head_spec(tok), head_spec(tok), row_spec(), row_spec(), row_spec()],
        [(EDGE, width), (2, tok, width)],
        [head_spec(EDGE), head_spec_3(2, tok)],
        "grads",
    )

    def neighbours(padded):
        nxt = passed_along(padded[:BLOCK].astype(jnp.bfloat16), "seq", -1)
        prev = passed_along(padded[tok + BLOCK :].astype(jnp.bfloat16), "seq", 1)
        return nxt, prev

    near_v = neighbours(value_padded)
    near_k = neighbours(key_padded)
    extra = jnp.concatenate([pieces(key_global), pieces(edge_dq)], axis=1)
    send_k = send_k.at[:, filled:].set(extra)
    send_k, returned_v = lax.optimization_barrier((send_k, returned_v))
    returned_k = exchange(send_k)
    (dv,) = final(
        final_value_kernel, 1, capacity, place, served,
        (returned_v, value_padded, local, *near_v), (), per_dev, "final_value",
    )

    def summed(block):
        return jnp.sum(block.astype(jnp.float32), axis=0).astype(jnp.bfloat16).reshape(share, width)

    def collected(first, second, number):
        got = collect(jnp.concatenate([first, second]).reshape(16, -1), owners, number)
        return got.reshape(owners, 2, share, width).transpose(1, 0, 2, 3).reshape(2, EDGE, width)

    returned_v, dv = lax.optimization_barrier((returned_v, dv))
    global_v, edge_out = collected(summed(returned_v[:, filled:]), out_row.reshape(share, width), 1)
    returned_k, dv, global_v, edge_out = lax.optimization_barrier(
        (returned_k, dv, global_v, edge_out)
    )
    count = share * width // HD
    global_k, edge_dq = collected(
        summed(returned_k[:, filled : filled + count]), summed(returned_k[:, filled + count :]), 2
    )
    dk, att, dq, dv, gain_term = final(
        final_key_kernel, 0, capacity, place, served,
        (returned_k, key_padded, local, *near_k),
        (
            global_k, global_v, edge_dq, edge_out, keys[0], key_gain[None], att, dq, dv,
        ),
        per_dev, "final_key",
    )
    gain_grad = lax.psum(jnp.sum(to_all(gain_term), axis=(0, 1)), "dp")
    return att[None], dq[None], dk[None], dv[None], gain_grad


def solution(mesh):
    placed = (
        P("dp", "seq", None),
        P("dp", "seq", None),
        P("dp", "seq", None),
        P(),
        P(None, "seq", None),
        P("dp", "seq", None),
    )
    return jax.shard_map(
        shards,
        mesh=mesh,
        in_specs=placed,
        out_specs=(
            P("dp", "seq", None),
            P("dp", "seq", None),
            P("dp", "seq", None),
            P("dp", "seq", None),
            P(),
        ),
        check_vma=False,
    )
```

```python
import functools

import jax
import jax.numpy as jnp
from jax import lax
from jax.experimental import pallas as pl
from jax.experimental.pallas import tpu as pltpu
from jax.sharding import PartitionSpec as P

HEADS = 16
HD = 128
BLOCK = 64
NG = 2
NR = 3
NK = 8
EDGE = NG * BLOCK
SCALE = HD ** (-0.5)
NEGATIVE = -1e30
VMEM = pltpu.CompilerParams(vmem_limit_bytes=56 * 1024 * 1024)
WHOLE = pl.BlockSpec(memory_space=pltpu.VMEM)


def dot_nt(a, b):
    return lax.dot_general(a, b, (((1,), (1,)), ((), ())), preferred_element_type=jnp.float32)


def dot_nn(a, b):
    return lax.dot_general(a, b, (((1,), (0,)), ((), ())), preferred_element_type=jnp.float32)


def dot_tn(a, b):
    return lax.dot_general(a, b, (((0,), (0,)), ((), ())), preferred_element_type=jnp.float32)


def passed_along(array, axis, by):
    length = lax.axis_size(axis)
    pairs = [(i, i + by) for i in range(length) if 0 <= i + by < length]
    return lax.ppermute(array, axis, pairs)


def on(device):
    return dict(device_id={"seq": device}, device_id_type=pl.DeviceIdType.MESH)


def spread_kernel(count, in_ref, out_ref, send_sem, recv_sem):
    me = lax.axis_index("seq")
    children = (
        ((lax.rem(me, 8) == 0) & (me + 8 < count), 8),
        (lax.rem(me, 8) == 0, 4),
        (lax.rem(me, 4) == 0, 2),
        (lax.rem(me, 2) == 0, 1),
    )
    near = jnp.where(lax.rem(me, 4) == 2, me - 2, jnp.where(lax.rem(me, 8) == 4, me - 4, me - 8))
    parent = jnp.where(lax.rem(me, 2) == 1, me - 1, near)
    barrier = pltpu.get_barrier_semaphore()
    greeted = jnp.where(me > 0, 1, 0)
    for there, step in children:
        greeted = greeted + jnp.where(there, 1, 0)

        @pl.when(there)
        def _():
            pl.semaphore_signal(barrier, inc=1, **on(me + step))

    @pl.when(me > 0)
    def _():
        pl.semaphore_signal(barrier, inc=1, **on(parent))

    pl.semaphore_wait(barrier, greeted)

    @pl.when(me == 0)
    def _():
        out_ref[...] = in_ref[...]

    def copy(c, i, device):
        return pltpu.make_async_remote_copy(
            src_ref=out_ref.at[c],
            dst_ref=out_ref.at[c],
            send_sem=send_sem.at[i, c],
            recv_sem=recv_sem.at[c],
            **on(device),
        )

    def forward(c, carry):
        @pl.when(me > 0)
        def _():
            copy(c, 0, parent).wait_recv()

        for i, (there, step) in enumerate(children):

            @pl.when(there)
            def _():
                copy(c, i, me + step).start()

        return carry

    def finish(c, carry):
        for i, (there, step) in enumerate(children):

            @pl.when(there)
            def _():
                copy(c, i, me + step).wait_send()

        return carry

    lax.fori_loop(0, out_ref.shape[0], forward, 0)
    lax.fori_loop(0, out_ref.shape[0], finish, 0)


def spread(array, count):
    chunks = array.shape[0]
    return pl.pallas_call(
        functools.partial(spread_kernel, count),
        in_specs=[WHOLE],
        out_specs=WHOLE,
        out_shape=jax.ShapeDtypeStruct(array.shape, array.dtype),
        scratch_shapes=[
            pltpu.SemaphoreType.DMA((4, chunks)),
            pltpu.SemaphoreType.DMA((chunks,)),
        ],
        compiler_params=pltpu.CompilerParams(
            collective_id=0, has_side_effects=True, vmem_limit_bytes=32 * 1024 * 1024
        ),
        name="spread",
    )(array)


def collect_kernel(count, in_ref, out_ref, send_sem, recv_sem):
    me = lax.axis_index("seq")
    barrier = pltpu.get_barrier_semaphore()

    def copy(device):
        return pltpu.make_async_remote_copy(
            src_ref=in_ref,
            dst_ref=out_ref.at[device],
            send_sem=send_sem,
            recv_sem=recv_sem.at[device],
            **on(0),
        )

    @pl.when(me == 0)
    def _():
        def greet(d, carry):
            pl.semaphore_signal(barrier, inc=1, **on(d))
            return carry

        lax.fori_loop(1, count, greet, 0)
        pl.semaphore_wait(barrier, count - 1)
        out_ref[0] = in_ref[...]

        def receive(d, carry):
            copy(d).wait_recv()
            return carry

        lax.fori_loop(1, count, receive, 0)

    @pl.when(me > 0)
    def _():
        pl.semaphore_signal(barrier, inc=1, **on(0))
        pl.semaphore_wait(barrier, 1)
        copy(me).start()
        copy(me).wait_send()


def collect(piece, count, number):
    return pl.pallas_call(
        functools.partial(collect_kernel, count),
        in_specs=[WHOLE],
        out_specs=WHOLE,
        out_shape=jax.ShapeDtypeStruct((count,) + piece.shape, piece.dtype),
        scratch_shapes=[pltpu.SemaphoreType.DMA, pltpu.SemaphoreType.DMA((count,))],
        compiler_params=pltpu.CompilerParams(
            collective_id=number, has_side_effects=True, vmem_limit_bytes=32 * 1024 * 1024
        ),
        name=f"collect_{number}",
    )(piece)


def slot_rows(slot, capacity):
    start = pl.multiple_of(lax.rem(slot, capacity) * BLOCK, BLOCK)
    return lax.div(slot, capacity), pl.ds(start, BLOCK)


def pick_kernel(
    per_dev, capacity, index_ref, key_ref, value_ref, extra_ref, key_out, value_out
):
    filled = capacity * BLOCK
    key_out[:, filled:, :] = extra_ref[...]
    value_out[:, filled:, :] = jnp.zeros_like(value_out[:, filled:, :])

    def step(s, carry):
        table = jnp.maximum(index_ref[s], 0)
        rows = pl.ds(pl.multiple_of(lax.rem(table, per_dev) * BLOCK, BLOCK), BLOCK)
        cols = pl.ds(pl.multiple_of(lax.div(table, per_dev) * HD, HD), HD)
        owner, place = slot_rows(s, capacity)
        key_out[owner, place, :] = key_ref[rows, cols]
        value_out[owner, place, :] = value_ref[rows, cols]
        return carry

    lax.fori_loop(0, key_out.shape[0] * capacity, step, 0, unroll=4)


def pick(index, key_eff, values, extra, more, per_dev, capacity):
    owners = extra.shape[0]
    filled = capacity * BLOCK
    return pl.pallas_call(
        functools.partial(pick_kernel, per_dev, capacity),
        grid_spec=pltpu.PrefetchScalarGridSpec(
            num_scalar_prefetch=1, grid=(), in_specs=[WHOLE] * 3, out_specs=[WHOLE, WHOLE]
        ),
        out_shape=[
            jax.ShapeDtypeStruct((owners, filled + extra.shape[1], HD), jnp.bfloat16),
            jax.ShapeDtypeStruct((owners, filled + more, HD), jnp.bfloat16),
        ],
        compiler_params=VMEM,
        name="pick",
    )(index, key_eff, values, extra)


def in_parts(x):
    high = lax.reduce_precision(x, 8, 7)
    middle = lax.reduce_precision(x - high, 8, 7)
    return jnp.stack([high, middle, x - high - middle]).astype(jnp.bfloat16)


def from_parts(parts, axis):
    parts = parts.astype(jnp.float32)
    low = [lax.index_in_dim(parts, i, axis, keepdims=False) for i in range(3)]
    return low[0] + (low[1] + low[2])


def listed_rows(edge_rows, window_rows, p, arrived_ref, slots):
    window = window_rows[p * BLOCK : (p + 3) * BLOCK]
    return jnp.concatenate([edge_rows, window] + [arrived_ref[s[0], s[1], :] for s in slots], axis=0)


def softmax_parts(q, keys, block, total_blocks):
    column = lax.broadcasted_iota(jnp.int32, (1, NK * BLOCK), 1)
    listed = block - 1 - NG + column // BLOCK
    mask = (column < EDGE) | (column >= EDGE + 3 * BLOCK)
    mask = mask | ((listed >= NG) & (listed < total_blocks))
    scores = jnp.where(mask, dot_nt(q, keys) * SCALE, NEGATIVE)
    top = jnp.max(scores, axis=1, keepdims=True)
    expo = jnp.where(mask, jnp.exp(scores - top), 0.0)
    total = jnp.sum(expo, axis=1, keepdims=True)
    keep = jnp.where(block >= NG, 1.0, 0.0).astype(jnp.float32)
    return expo, total, expo * (keep / total)


def scatter_terms(terms, p, slots, global_ref, padded_ref, send_ref):
    global_ref[...] += terms[:EDGE]
    padded_ref[p * BLOCK : (p + 3) * BLOCK, :] += terms[EDGE : EDGE + 3 * BLOCK]
    for r in range(NR):
        start = EDGE + (3 + r) * BLOCK
        send_ref[slots[r][0], slots[r][1], :] = terms[start : start + BLOCK].astype(jnp.bfloat16)


def clear(head, global_ref, padded_ref, send_ref):
    @pl.when(head == 0)
    def _():
        send_ref[...] = jnp.zeros_like(send_ref)

    global_ref[...] = jnp.zeros_like(global_ref)
    padded_ref[...] = jnp.zeros_like(padded_ref)


def value_kernel(
    per_dev, capacity, place_ref, pos_ref, q_ref, g_ref, k_ref, left_ref, right_ref, edge_ref,
    arrived_ref, global_ref, padded_ref, send_ref,
):
    head = pl.program_id(0)
    clear(head, global_ref, padded_ref, send_ref)
    k_window = jnp.concatenate([left_ref[0], k_ref[...], right_ref[0]], axis=0)
    for p in range(per_dev):
        rows = slice(p * BLOCK, (p + 1) * BLOCK)
        slots = [
            slot_rows(pos_ref[(head * per_dev + p) * NR + r], capacity) for r in range(NR)
        ]
        keys = listed_rows(edge_ref[1], k_window, p, arrived_ref, slots)
        _, _, weights = softmax_parts(q_ref[rows, :], keys, place_ref[0] + p, place_ref[1])
        terms = dot_tn(weights.astype(jnp.bfloat16), g_ref[rows, :])
        scatter_terms(terms, p, slots, global_ref, padded_ref, send_ref)


def key_kernel(
    per_dev, capacity, place_ref, pos_ref, q_ref, g_ref, k_ref, left_ref, right_ref, edge_ref,
    arrived_ref, v_ref, arrived_v_ref, global_ref, padded_ref, send_ref, att_ref, dq_ref,
):
    head = pl.program_id(0)
    clear(head, global_ref, padded_ref, send_ref)
    k_window = jnp.concatenate([left_ref[0], k_ref[...], right_ref[0]], axis=0)
    v_window = jnp.concatenate([left_ref[1], v_ref[...], right_ref[1]], axis=0)
    for p in range(per_dev):
        rows = slice(p * BLOCK, (p + 1) * BLOCK)
        slots = [
            slot_rows(pos_ref[(head * per_dev + p) * NR + r], capacity) for r in range(NR)
        ]
        keys = listed_rows(edge_ref[1], k_window, p, arrived_ref, slots)
        values = listed_rows(edge_ref[2], v_window, p, arrived_v_ref, slots)
        q = q_ref[rows, :]
        g = g_ref[rows, :]
        expo, total, weights = softmax_parts(q, keys, place_ref[0] + p, place_ref[1])
        attended = (dot_nn(expo.astype(jnp.bfloat16), values) / total).astype(jnp.bfloat16)
        delta = jnp.sum(
            g.astype(jnp.float32) * attended.astype(jnp.float32), axis=1, keepdims=True
        )
        dscores = (weights * (dot_nt(g, values) - delta) * SCALE).astype(jnp.bfloat16)
        att_ref[rows, :] = attended
        dq_ref[rows, :] = dot_nn(dscores, keys).astype(jnp.bfloat16)
        scatter_terms(dot_tn(dscores, q), p, slots, global_ref, padded_ref, send_ref)


def head_spec(rows):
    return pl.BlockSpec((rows, HD), lambda h, *_: (0, h))


def head_spec_3(parts, rows):
    return pl.BlockSpec((parts, rows, HD), lambda h, *_: (0, 0, h))


def row_spec():
    return pl.BlockSpec((1, 1, EDGE), lambda h, *_: (h, 0, 0))


def sparse(kernel, place, position, inputs, more, per_dev, capacity, extra, outs, name):
    q = inputs[0]
    tok = q.shape[0]
    width = q.shape[1]
    wide = tok + 2 * BLOCK
    slots = (inputs[6].shape[0], capacity * BLOCK + extra, HD)
    return pl.pallas_call(
        functools.partial(kernel, per_dev, capacity),
        grid_spec=pltpu.PrefetchScalarGridSpec(
            num_scalar_prefetch=2,
            grid=(HEADS,),
            in_specs=[head_spec(tok)] * 3
            + [head_spec_3(2, BLOCK)] * 2
            + [head_spec_3(4, EDGE), WHOLE]
            + [head_spec(tok), WHOLE][: len(more)],
            out_specs=[head_spec(EDGE), head_spec(wide), WHOLE] + [head_spec(tok)] * outs,
        ),
        out_shape=[
            jax.ShapeDtypeStruct((EDGE, width), jnp.float32),
            jax.ShapeDtypeStruct((wide, width), jnp.float32),
            jax.ShapeDtypeStruct(slots, jnp.bfloat16),
        ]
        + [jax.ShapeDtypeStruct((tok, width), jnp.bfloat16)] * outs,
        compiler_params=VMEM,
        name=name,
    )(place, position, *inputs, *more)


def edge_sum_kernel(edge_ref, k_ref, v_ref, top_ref, total_ref, numer_ref):
    scores = dot_nt(k_ref[...], edge_ref[0]) * SCALE
    top = jnp.max(scores, axis=0, keepdims=True)
    expo = jnp.exp(scores - top)
    top_ref[0] = top
    total_ref[0] = jnp.sum(expo, axis=0, keepdims=True)
    numer_ref[...] = dot_tn(expo.astype(jnp.bfloat16), v_ref[...])


def edge_grad_kernel(edge_ref, k_ref, v_ref, top_ref, total_ref, delta_ref, dq_ref, dkv_ref):
    q = edge_ref[0]
    g = edge_ref[3]
    scores = dot_nt(k_ref[...], q) * SCALE
    weights = jnp.exp(scores - top_ref[0]) / total_ref[0]
    dprobs = dot_nt(v_ref[...], g)
    dscores = (weights * (dprobs - delta_ref[0]) * SCALE).astype(jnp.bfloat16)
    dq_ref[...] = dot_tn(dscores, k_ref[...])
    dkv_ref[0] = dot_nn(dscores, q)
    dkv_ref[1] = dot_nn(weights.astype(jnp.bfloat16), g)


def edge_call(kernel, inputs, specs, outs, out_specs, name):
    return pl.pallas_call(
        kernel,
        grid=(HEADS,),
        in_specs=specs,
        out_specs=out_specs,
        out_shape=[jax.ShapeDtypeStruct(s, jnp.float32) for s in outs],
        compiler_params=VMEM,
        name=name,
    )(*inputs)


def sum_terms(
    per_dev, capacity, place_ref, served_ref, returned_ref, padded_ref, local_ref, next_ref,
    prev_ref, global_ref, acc_ref,
):
    head = pl.program_id(0)

    @pl.when(head == 0)
    def _():
        acc_ref[...] = jnp.zeros_like(acc_ref)

        def step(s, carry):
            table = served_ref[s]

            @pl.when(table >= 0)
            def _():
                owner, rows = slot_rows(s, capacity)
                acc_ref[table] += returned_ref[owner, rows, :].astype(jnp.float32)

            return carry

        lax.fori_loop(0, returned_ref.shape[0] * capacity, step, 0)

    sums = []
    for p in range(per_dev):
        rows = slice(p * BLOCK, (p + 1) * BLOCK)
        shifted = slice((p + 1) * BLOCK, (p + 2) * BLOCK)
        term = padded_ref[shifted, :] + local_ref[0, rows, :] + acc_ref[head * per_dev + p]
        if p == per_dev - 1:
            term = term + next_ref[...].astype(jnp.float32)
        if p == 0:
            term = term + prev_ref[...].astype(jnp.float32)
        if global_ref is not None and p < NG:
            whole = global_ref[rows, :].astype(jnp.float32)
            term = term + jnp.where(place_ref[0] == 0, whole, 0.0)
        sums.append(term)
    return sums


def final_value_kernel(
    per_dev, capacity, place_ref, served_ref, returned_ref, padded_ref, local_ref, next_ref,
    prev_ref, dv_out, acc_ref,
):
    sums = sum_terms(
        per_dev, capacity, place_ref, served_ref, returned_ref, padded_ref, local_ref, next_ref,
        prev_ref, None, acc_ref,
    )
    for p in range(per_dev):
        dv_out[p * BLOCK : (p + 1) * BLOCK, :] = sums[p]


def final_key_kernel(
    per_dev, capacity, place_ref, served_ref, returned_ref, padded_ref, local_ref, next_ref,
    prev_ref, gk_ref, gv_ref, edq_ref, eout_ref, keys_ref, gain_ref, att_ref, dq_ref, dv_ref,
    dk_out, att_out, dq_out, dv_out, gain_out, acc_ref,
):
    sums = sum_terms(
        per_dev, capacity, place_ref, served_ref, returned_ref, padded_ref, local_ref, next_ref,
        prev_ref, gk_ref, acc_ref,
    )
    is_edge = place_ref[0] == 0
    gain_sum = jnp.zeros((1, HD), jnp.float32)
    for p in range(per_dev):
        rows = slice(p * BLOCK, (p + 1) * BLOCK)
        dk_out[rows, :] = (sums[p] * gain_ref[...]).astype(jnp.bfloat16)
        gain_sum = gain_sum + jnp.sum(
            sums[p] * keys_ref[rows, :].astype(jnp.float32), axis=0, keepdims=True
        )
        if p < NG:
            att_out[rows, :] = jnp.where(is_edge, eout_ref[rows, :], att_ref[rows, :])
            dq_out[rows, :] = jnp.where(is_edge, edq_ref[rows, :], dq_ref[rows, :])
            whole = jnp.where(is_edge, gv_ref[rows, :].astype(jnp.float32), 0.0)
            dv_out[rows, :] = (dv_ref[rows, :] + whole).astype(jnp.bfloat16)
        else:
            dv_out[rows, :] = dv_ref[rows, :].astype(jnp.bfloat16)
            att_out[rows, :] = att_ref[rows, :]
            dq_out[rows, :] = dq_ref[rows, :]
    gain_out[...] = gain_sum


def final(kernel, part, capacity, place, served, inputs, more, per_dev, name):
    tok = inputs[2].shape[1]
    width = inputs[2].shape[2]
    more_specs = [head_spec(x.shape[0]) for x in more]
    outs = [jax.ShapeDtypeStruct((tok, width), jnp.float32)]
    if more:
        outs = [jax.ShapeDtypeStruct((tok, width), jnp.bfloat16)] * 4
        outs = outs + [jax.ShapeDtypeStruct((1, width), jnp.float32)]
    return pl.pallas_call(
        functools.partial(kernel, per_dev, capacity),
        grid_spec=pltpu.PrefetchScalarGridSpec(
            num_scalar_prefetch=2,
            grid=(HEADS,),
            in_specs=[
                WHOLE,
                head_spec(tok + 2 * BLOCK),
                pl.BlockSpec((1, tok, HD), lambda h, *_: (part, 0, h)),
                head_spec(BLOCK),
                head_spec(BLOCK),
            ]
            + more_specs,
            out_specs=[head_spec(x.shape[0]) for x in outs],
            scratch_shapes=[pltpu.VMEM((HEADS * per_dev, BLOCK, HD), jnp.float32)],
        ),
        out_shape=outs,
        compiler_params=VMEM,
        name=name,
    )(place, served, *inputs, *more)


def shards(queries, keys, values, key_gain, random_blocks, out_grad):
    tok = queries.shape[1]
    width = queries.shape[2]
    per_dev = tok // BLOCK
    owners = lax.axis_size("seq")
    seq_place = lax.axis_index("seq")
    first_block = seq_place * per_dev
    place = jnp.stack([first_block, jnp.int32(owners * per_dev)]).astype(jnp.int32)
    q, v, g = queries[0], values[0], out_grad[0]
    key_eff = (keys[0].astype(jnp.float32) * key_gain).astype(jnp.bfloat16)

    request_count = HEADS * per_dev * NR
    capacity = (request_count + owners - 1) // owners + 3
    target = random_blocks.reshape(request_count)
    owner_dev = target // per_dev
    table_index = (
        jnp.arange(request_count, dtype=jnp.int32) // (per_dev * NR) * per_dev + target % per_dev
    )
    onehot = (owner_dev[:, None] == jnp.arange(owners, dtype=jnp.int32)[None, :]).astype(jnp.int32)
    before = jnp.cumsum(onehot, axis=0) - onehot
    slot_rank = jnp.sum(before * onehot, axis=1)
    position = (owner_dev * capacity + slot_rank).astype(jnp.int32)
    hit = position[:, None] == jnp.arange(owners * capacity, dtype=jnp.int32)[None, :]
    outgoing = (
        jnp.sum(jnp.where(hit, table_index[:, None] + 1, 0), axis=0).astype(jnp.int32) - 1
    ).reshape(owners, capacity)
    served = lax.all_to_all(outgoing, "seq", split_axis=0, concat_axis=0, tiled=True)
    served = served.reshape(owners * capacity)
    filled = capacity * BLOCK

    def exchange(slots):
        return lax.all_to_all(slots, "seq", split_axis=0, concat_axis=0, tiled=True)

    def to_all(array):
        spread_out = jnp.broadcast_to(array[None], (owners,) + array.shape)
        return lax.all_to_all(spread_out, "seq", split_axis=0, concat_axis=0, tiled=True)

    def pieces(rows):
        return rows.astype(jnp.bfloat16).reshape(owners, -1, HD)

    def padded_rows(flat, count):
        flat = jnp.pad(flat, ((0, 0), (0, count * HD - flat.shape[1])))
        return flat.reshape(flat.shape[0], count, HD)

    edge = jnp.stack([q[:EDGE], key_eff[:EDGE], v[:EDGE], g[:EDGE]])
    edge = spread(edge.reshape(32, 4 * EDGE // 32, width), owners).reshape(4, EDGE, width)
    tails = jnp.stack([key_eff[tok - BLOCK :], v[tok - BLOCK :]])
    heads = jnp.stack([key_eff[:BLOCK], v[:BLOCK]])
    left = passed_along(tails, "seq", 1)
    right = passed_along(heads, "seq", -1)

    stat = (HEADS, 1, EDGE)
    edge_in = head_spec_3(4, EDGE)
    top, total, numer = edge_call(
        edge_sum_kernel,
        (edge, key_eff, v),
        [edge_in, head_spec(tok), head_spec(tok)],
        [stat, stat, (EDGE, width)],
        [row_spec(), row_spec(), head_spec(EDGE)],
        "sums",
    )
    share = EDGE // owners
    stats = in_parts(jnp.concatenate([top[:, 0], total[:, 0]])).transpose(2, 0, 1)
    stats = padded_rows(stats.reshape(owners, share * 6 * HEADS), 16)
    extra = jnp.concatenate([pieces(numer), stats], axis=1)
    picked_k, picked_v = pick(served, key_eff, v, extra, 16, per_dev, capacity)
    picked_k, left, right = lax.optimization_barrier((picked_k, left, right))
    arrived_k = exchange(picked_k)
    parts = arrived_k[:, filled : filled + share * width // HD]
    parts = parts.reshape(owners, share, HEADS, HD).astype(jnp.float32)
    stats = arrived_k[:, filled + share * width // HD :].reshape(owners, -1)
    stats = stats[:, : share * 6 * HEADS].reshape(owners, share, 3, 2 * HEADS)
    stats = from_parts(stats, 2)
    tops = stats[:, :, :HEADS]
    top_row = jnp.max(tops, axis=0)
    factor = jnp.exp(tops - top_row[None])
    total_row = jnp.sum(factor * stats[:, :, HEADS:], axis=0)
    numer_row = jnp.sum(parts * factor[..., None], axis=0)
    out_row = (numer_row / total_row[..., None]).astype(jnp.bfloat16)
    grad_row = lax.dynamic_slice_in_dim(edge[3], seq_place * share, share, axis=0)
    grad_row = grad_row.reshape(share, HEADS, HD).astype(jnp.float32)
    delta_row = jnp.sum(grad_row * out_row.astype(jnp.float32), axis=2)
    row_stats = in_parts(jnp.stack([top_row, total_row, delta_row]))
    row_stats = padded_rows(row_stats.reshape(1, 9 * share * HEADS), 16)
    picked_v = picked_v.at[:, filled:].set(jnp.broadcast_to(row_stats, (owners, 16, HD)))
    arrived_v = exchange(picked_v)

    base = [q, g, key_eff, left, right, edge, arrived_k]
    value_global, value_padded, send_v = sparse(
        value_kernel, place, position, base, [], per_dev, capacity, share * width // HD, 0,
        "value_terms",
    )
    arrived_v, send_v, value_global = lax.optimization_barrier((arrived_v, send_v, value_global))
    row_stats = arrived_v[:, filled:].reshape(owners, -1)[:, : 9 * share * HEADS]
    row_stats = from_parts(row_stats.reshape(owners, 3, 3, share, HEADS), 1)
    row_stats = row_stats.transpose(1, 3, 0, 2).reshape(3, HEADS, 1, EDGE)
    returned_v = exchange(send_v.at[:, filled:].set(pieces(value_global)))
    key_global, key_padded, send_k, att, dq = sparse(
        key_kernel, place, position, base, [v, arrived_v], per_dev, capacity,
        2 * share * width // HD, 2, "key_terms",
    )
    edge_dq, local = edge_call(
        edge_grad_kernel,
        (edge, key_eff, v, row_stats[0], row_stats[1], row_stats[2]),
        [edge_in, head_spec(tok), head_spec(tok), row_spec(), row_spec(), row_spec()],
        [(EDGE, width), (2, tok, width)],
        [head_spec(EDGE), head_spec_3(2, tok)],
        "grads",
    )

    def neighbours(padded):
        nxt = passed_along(padded[:BLOCK].astype(jnp.bfloat16), "seq", -1)
        prev = passed_along(padded[tok + BLOCK :].astype(jnp.bfloat16), "seq", 1)
        return nxt, prev

    near_v = neighbours(value_padded)
    near_k = neighbours(key_padded)
    extra = jnp.concatenate([pieces(key_global), pieces(edge_dq)], axis=1)
    send_k = send_k.at[:, filled:].set(extra)
    send_k, returned_v = lax.optimization_barrier((send_k, returned_v))
    returned_k = exchange(send_k)
    (dv,) = final(
        final_value_kernel, 1, capacity, place, served,
        (returned_v, value_padded, local, *near_v), (), per_dev, "final_value",
    )

    def summed(block):
        return jnp.sum(block.astype(jnp.float32), axis=0).astype(jnp.bfloat16).reshape(share, width)

    returned_k, dv = lax.optimization_barrier((returned_k, dv))
    count = share * width // HD
    piece = jnp.concatenate(
        [
            summed(returned_k[:, filled : filled + count]),
            summed(returned_v[:, filled:]),
            summed(returned_k[:, filled + count :]),
            out_row.reshape(share, width),
        ]
    )
    got = collect(piece, owners, 1).reshape(owners, 4, share, width)
    global_k, global_v, edge_dq, edge_out = got.transpose(1, 0, 2, 3).reshape(4, EDGE, width)
    dk, att, dq, dv, gain_term = final(
        final_key_kernel, 0, capacity, place, served,
        (returned_k, key_padded, local, *near_k),
        (
            global_k, global_v, edge_dq, edge_out, keys[0], key_gain[None], att, dq, dv,
        ),
        per_dev, "final_key",
    )
    gain_grad = lax.psum(jnp.sum(to_all(gain_term), axis=(0, 1)), "dp")
    return att[None], dq[None], dk[None], dv[None], gain_grad


def solution(mesh):
    placed = (
        P("dp", "seq", None),
        P("dp", "seq", None),
        P("dp", "seq", None),
        P(),
        P(None, "seq", None),
        P("dp", "seq", None),
    )
    return jax.shard_map(
        shards,
        mesh=mesh,
        in_specs=placed,
        out_specs=(
            P("dp", "seq", None),
            P("dp", "seq", None),
            P("dp", "seq", None),
            P("dp", "seq", None),
            P(),
        ),
        check_vma=False,
    )
```
